128 devices in a mesh: ctx: 16 (over y_lo, z, core), tp: 8 (over y_hi, x).
Axes of the slice: x: 4, y: 4 (y_hi: 2, y_lo: 2; y = y_hi * 2 + y_lo), z: 4, core: 2. Of those that a mesh axis runs over, the one named last changes fastest.
Arguments:
- tokens: bfloat16 [4096, 16384], P('tp', 'ctx'), may hold values from -6 to 6
- in_weight: bfloat16 [3, 4096, 4096], P(None, 'ctx', 'tp'), may hold values from -0.09375 to 0.09375
- short_taps: float32 [3, 4096, 3], P(None, 'tp'), may hold values from -3 to 3
- long_filter: float32 [4096, 16384], P('tp', 'ctx'), may hold values from -2 to 2
- skip_gain: float32 [4096], P('tp'), may hold values from -4 to 4
- out_weight: bfloat16 [4096, 4096], P('tp', 'ctx'), may hold values from -0.125 to 0.125
Outputs:
- layer_out: bfloat16 [4096, 16384], P('tp', 'ctx')
The draws below stay inside these ranges and needn't reach their ends.
All inputs are finite; a program needn't handle non-finite values.
Results may differ from the reference program's by a relative error of at most 0.02.
Values may be sent and summed in bfloat16 or wider, within the bound.
A program may use at most 128 MiB of HBM per device.

```python
import math
import jax
import jax.numpy as jnp
from jax import lax

D = 4096
TAPS = 3
TOKENS = 16384
BLOCKS = 8


def draw_long_filter(key, part):
    key_rate, key_pick, key_noise = jax.random.split(key, 3)
    position = jnp.arange(TOKENS, dtype=jnp.float32)[None, :]
    pick = jax.random.uniform(key_pick, (D, 1), dtype=jnp.float32)
    blend = jax.random.uniform(key_rate, (D, 1), dtype=jnp.float32)
    slow_log = math.log(1.0 / (8.0 * TOKENS)) + blend * math.log(8.0)
    fast_log = math.log(1.0 / 50.0) + blend * math.log(50.0 / 30.0)
    slow_share = 0.5
    noise = jax.random.normal(key_noise, (D, TOKENS), dtype=jnp.float32)
    rates = jnp.exp(jnp.where(pick < slow_share, slow_log, fast_log))
    amplitude = jnp.sqrt(1.0 - jnp.exp(-2.0 * rates))
    values = noise * amplitude * jnp.exp(-rates * position)
    return jnp.clip(values, -2.0, 2.0).astype(jnp.float32)


def raised(drawn, own_key, source, target, parts, factor):
    def block_of(dim):
        return (jnp.arange(drawn.shape[dim]) // (drawn.shape[dim] // parts)).reshape((-1,) + (1,) * (drawn.ndim - 1 - dim))

    one_side = jax.random.permutation(own_key, parts)[block_of(target)]
    far = (block_of(target) + parts // 2) % parts
    return jnp.where((block_of(source) == one_side) | (block_of(source) == far), factor * drawn, drawn)


def levels(own_key, extent, shards, low, largest):
    factor_of = 1.0
    for dim, shards_of in shards:
        heights = jax.random.uniform(jax.random.fold_in(jax.random.fold_in(own_key, 6), dim), (shards_of,), jnp.float32, low / len(shards), largest / len(shards))
        factor_of = factor_of * jnp.repeat(jnp.exp(heights), extent[dim] // shards_of).reshape((-1,) + (1,) * (len(extent) - 1 - dim))
    return factor_of


def centred(own_key, dims, width, reach, cuts=(), held_as=jnp.bfloat16):
    values = width * jax.random.normal(own_key, dims, jnp.float32)
    if cuts:
        values = values * levels(own_key, dims, cuts, -0.22, 0.18)
    return jnp.clip(values, -reach, reach).astype(held_as)


def gaussian_with(stream_key, dims, scale, limit, pieces, heavy, kind=jnp.bfloat16):
    drawn = scale * jax.random.normal(stream_key, dims, jnp.float32)
    if pieces:
        drawn = drawn * levels(stream_key, dims, pieces, -0.22, 0.18)
    return jnp.clip(raised(drawn, jax.random.fold_in(stream_key, 3), *heavy), -limit, limit).astype(kind)


def setup_inputs(seed: int = 0) -> dict:
    key_of = jax.random.split(jax.random.key(seed), 7)
    tokens = centred(key_of[0], (D, TOKENS), 1.0, 6.0, ((0, 8), (1, 16)))
    in_weight = centred(key_of[1], (3, D, D), D ** -0.5, 0.09375, ((1, 16), (2, 8)))
    short_taps = centred(key_of[2], (3, D, TAPS), 0.6, 3.0, ((1, 8),), jnp.float32)
    long_filter = draw_long_filter(jax.random.fold_in(key_of[6], 71), 0)
    skip_gain = centred(key_of[4], (D,), 0.7, 4.0, ((0, 8),), jnp.float32)
    out_weight = gaussian_with(key_of[5], (D, D), D ** -0.5, 0.125, ((0, 8), (1, 16)), (0, 1, 16, 2.0))
    return {"tokens": tokens, "in_weight": in_weight, "short_taps": short_taps, "long_filter": long_filter, "skip_gain": skip_gain, "out_weight": out_weight}


def reference(tokens, in_weight, short_taps, long_filter, skip_gain, out_weight):
    streams = []
    for stream_id in range(3):
        streams.append(jnp.dot(in_weight[stream_id].T, tokens, preferred_element_type=jnp.float32))
    projected = jnp.stack(streams)
    padded = jnp.pad(projected, ((0, 0), (0, 0), (2, 0)))
    mixed_short = (short_taps[:, :, 0:1] * padded[:, :, 2:]
                   + short_taps[:, :, 1:2] * padded[:, :, 1:-1]
                   + short_taps[:, :, 2:3] * padded[:, :, :-2])
    gated_rows = (mixed_short[1] * mixed_short[2]).astype(jnp.bfloat16)
    spec_len = 2 * TOKENS
    sig_freq = jnp.fft.rfft(gated_rows.astype(jnp.float32), n=spec_len, axis=1)
    fil_freq = jnp.fft.rfft(long_filter, n=spec_len, axis=1)
    long_rows = jnp.fft.irfft(sig_freq * fil_freq, n=spec_len, axis=1)[:, :TOKENS].astype(jnp.bfloat16)
    hidden = ((long_rows.astype(jnp.float32) + skip_gain[:, None] * gated_rows.astype(jnp.float32))
              * mixed_short[0]).astype(jnp.bfloat16)
    rows_block = D // BLOCKS
    hidden_blocks = hidden.reshape(BLOCKS, rows_block, TOKENS)
    weight_blocks = out_weight.reshape(BLOCKS, rows_block, D)

    def add_block(running, block_id):
        block_term = jnp.dot(weight_blocks[block_id].T, hidden_blocks[block_id], preferred_element_type=jnp.float32)
        block_term = lax.optimization_barrier(block_term.astype(jnp.bfloat16))
        return running + block_term.astype(jnp.float32), block_id

    summed = lax.scan(add_block, jnp.zeros((D, TOKENS), jnp.float32), jnp.arange(BLOCKS, dtype=jnp.int32))[0]
    return summed.astype(jnp.bfloat16)
```

```python
import functools
import math

import jax
import jax.numpy as jnp
import numpy as np
from jax import lax
from jax.experimental import pallas as pl
from jax.experimental.pallas import tpu as pltpu
from jax.sharding import PartitionSpec as P

MESH = pl.DeviceIdType.MESH
BF16 = jnp.bfloat16
F32 = jnp.float32

RING = 4
PAIR = 2
CTX = 16
TP = 8
ROWS = 512
SLAB = 1024
WROWS = 256
OWN = 32
SIDE = 128
PART = 2
SUB = OWN // PART
HALF = ROWS // PART
BLOCK = SUB * 8

OWN_S, PAIR_S, LEFT, RIGHT, PLEFT, PRIGHT, FAR, PFAR = range(8)
COPIES = {
    "A": (0, OWN_S, PAIR_S, None, "pair"),
    "Bp": (1, OWN_S, LEFT, None, "plus"),
    "Bm": (2, OWN_S, RIGHT, None, "minus"),
    "Cp": (3, PAIR_S, PLEFT, None, "plus"),
    "Cm": (4, PAIR_S, PRIGHT, None, "minus"),
    "Dp": (5, LEFT, FAR, 0, "plus"),
    "Dm": (6, RIGHT, FAR, 1, "minus"),
    "Ep": (7, PLEFT, PFAR, 0, "plus"),
    "Em": (8, PRIGHT, PFAR, 1, "minus"),
    "AL": (3, LEFT, PLEFT, None, "pair"),
    "AR": (4, RIGHT, PRIGHT, None, "pair"),
    "AF0": (7, FAR, PFAR, 0, "pair"),
    "AF1": (8, FAR, PFAR, 1, "pair"),
}


def tables():
    i = np.arange(SIDE)
    quarter = 2 * np.pi * ((i[:, None] * (4 * i[None, :] + 1)) % (4 * SIDE)) / (4 * SIDE)
    plain = 2 * np.pi * ((i[:, None] * i[None, :]) % SIDE) / SIDE
    twist = 2 * np.pi * (((4 * i[:, None] + 1) * i[None, :]) % (4 * SIDE * SIDE)) / (4 * SIDE * SIDE)
    f1 = np.concatenate([np.cos(quarter.T), -np.sin(quarter.T)], 0)
    c, s = np.cos(plain), np.sin(plain)
    f2 = np.block([[c, -s], [s, c]])
    f3 = np.block([[c, s], [-s, c]])
    f4 = np.concatenate([np.cos(quarter), -np.sin(quarter)], 1) / (SIDE * SIDE)
    tw = np.stack([np.cos(twist), np.sin(twist)])
    return [jnp.asarray(a, BF16) for a in (f1, f2, f3, f4)] + [jnp.asarray(tw, F32)]


def rel_slot(dring, dpair):
    return 3 * dring - 7 * (dring // 3) + dpair * (1 + dring % 2)


class Gather:
    def __init__(self, devs, src, dst, got, send_sem, recv_sem):
        self.devs, self.src, self.dst, self.got = devs, src, dst, got
        self.send_sem, self.recv_sem = send_sem, recv_sem
        self.sent = []

    def send(self, *names):
        for name in names:
            i, shard, there, half, to = COPIES[name]
            copy = pltpu.make_async_remote_copy(
                src_ref=self.src(shard, half),
                dst_ref=self.dst(shard, there, half),
                send_sem=self.send_sem.at[i],
                recv_sem=self.recv_sem.at[i],
                device_id=self.devs[to],
                device_id_type=MESH,
            )
            copy.start()
            self.sent.append(copy)

    def recv(self, *names):
        for name in names:
            i, _, there, half, to = COPIES[name]
            ref = self.got(there, half)
            pltpu.make_async_copy(ref, ref, self.recv_sem.at[i]).wait()

    def finish(self):
        for copy in self.sent:
            copy.wait_send()


def dot(a, b):
    return jnp.dot(a, b, preferred_element_type=F32)


def kernel(
    tok, w, taps, filt, skip, ow, f1, f2, f3, f4, tw,
    out,
    tok_all, w_all, ow_all, hid_all, acc, w_st, ow_st, ow_send,
    fsend, frecv, gated, gsend, grecv, xf, spec, lsend, lrecv,
    halo_send, halo_recv, halo_t, rows_t, taps_t,
    local_sem, tok_ss, tok_rs, w_ss, w_rs, ow_ss, ow_rs, h_ss, h_rs, w_sib_ss, w_sib_rs, ow_sib_ss, ow_sib_rs,
    swap_sem, halo_sem, f_ss, f_rs, g_ss, g_rs, l_ss, l_rs,
):
    ctx, tp = lax.axis_index("ctx"), lax.axis_index("tp")
    y_lo, z, core = ctx // 8, (ctx // 2) % 4, ctx % 2
    y_hi, x = tp // 4, tp % 4

    def ctx_at(y, zz, c):
        return y * 8 + zz * 2 + c

    tp_devs = {
        "pair": (ctx, (1 - y_hi) * 4 + x),
        "plus": (ctx, y_hi * 4 + (x + 1) % 4),
        "minus": (ctx, y_hi * 4 + (x + 3) % 4),
    }
    ctx_devs = {
        "pair": (ctx_at(1 - y_lo, z, core), tp),
        "plus": (ctx_at(y_lo, (z + 1) % 4, core), tp),
        "minus": (ctx_at(y_lo, (z + 3) % 4, core), tp),
    }
    sibling = (ctx_at(y_lo, z, 1 - core), tp)
    swap_dev = (ctx_at(y_hi, x, core), y_lo * 4 + z)
    swap_here = (ctx // 2) == tp

    local = [
        pltpu.make_async_copy(w, w_st, local_sem.at[0]),
        pltpu.make_async_copy(ow, ow_st, local_sem.at[1]),
        pltpu.make_async_copy(filt, acc.at[0], local_sem.at[2]),
        pltpu.make_async_copy(tok, tok_all.at[pl.ds(0, ROWS)], local_sem.at[3]),
    ]
    for copy in local:
        copy.start()
    halo_recv[...] = jnp.zeros_like(halo_recv)

    barrier = pltpu.get_barrier_semaphore()
    for i in range(1, CTX):
        pl.semaphore_signal(barrier, inc=1, device_id=((ctx + i) % CTX, tp), device_id_type=MESH)
    for d in tp_devs.values():
        pl.semaphore_signal(barrier, inc=1, device_id=d, device_id_type=MESH)

    @pl.when(jnp.logical_not(swap_here))
    def _():
        pl.semaphore_signal(barrier, inc=1, device_id=swap_dev, device_id_type=MESH)
        pl.semaphore_wait(barrier, CTX + 3)

    @pl.when(swap_here)
    def _():
        pl.semaphore_wait(barrier, CTX + 2)

    def tok_src(shard, half):
        if shard == OWN_S:
            return tok
        return tok_dst(None, shard, half)

    def tok_dst(_, there, half):
        if half is None:
            return tok_all.at[pl.ds(there * ROWS, ROWS)]
        return tok_all.at[pl.ds(there * ROWS + half * HALF, HALF)]

    t_g = Gather(tp_devs, tok_src, tok_dst, lambda there, half: tok_dst(None, there, half), tok_ss, tok_rs)
    t_g.send("Bp", "Bm", "A")

    def w_slot(shard):
        dz = {OWN_S: 0, PAIR_S: 0, LEFT: 3, RIGHT: 1, PLEFT: 3, PRIGHT: 1, FAR: 2, PFAR: 2}[shard]
        dy = 1 if shard in (PAIR_S, PLEFT, PRIGHT, PFAR) else 0
        return rel_slot((z + dz + 4 - x) % 4, (y_lo + dy + y_hi) % 2)

    def w_view(shard, half, c=core):
        lanes = pl.ds(pl.multiple_of(w_slot(shard) * ROWS + c * WROWS, WROWS), WROWS)
        if half is None:
            return w_all.at[:, :, lanes]
        return w_all.at[:, pl.ds(half * HALF, HALF), lanes]

    w_g = Gather(ctx_devs, w_view, lambda shard, there, half: w_view(shard, half), w_view, w_ss, w_rs)

    def sib_copy(view, shard, ss, rs):
        return pltpu.make_async_remote_copy(
            src_ref=view(shard, None),
            dst_ref=view(shard, None),
            send_sem=ss.at[shard],
            recv_sem=rs.at[shard],
            device_id=sibling,
            device_id_type=MESH,
        )

    sib_sent = []

    def w_sib(shard):
        copy = sib_copy(w_view, shard, w_sib_ss, w_sib_rs)
        copy.start()
        sib_sent.append(copy)

    local[0].wait()
    for s in range(3):
        lanes = pl.ds(pl.multiple_of(w_slot(OWN_S) * ROWS + core * WROWS, WROWS), WROWS)
        w_all[s, :, lanes] = w_st[s].T
    w_g.send("Bp", "Bm", "A")
    w_sib(OWN_S)

    def ow_view(shard, half, c=core):
        lanes = pl.ds(pl.multiple_of(w_slot(shard) * HALF, HALF), HALF)
        rows = pl.ds(pl.multiple_of(c * WROWS, WROWS), WROWS)
        if half is None:
            return ow_all.at[:, rows, lanes]
        return ow_all.at[half, rows, lanes]

    local[1].wait()
    for h in range(PART):
        picked = jnp.concatenate([ow_st[pl.ds(d * OWN + h * SUB, SUB), :] for d in range(CTX)], axis=0)
        ow_send[h] = picked.T
    swap_lanes = pl.ds(pl.multiple_of(rel_slot((x + 4 - z) % 4, (y_hi + y_lo) % 2) * HALF, HALF), HALF)
    swap_rows = pl.ds(pl.multiple_of(core * WROWS, WROWS), WROWS)
    swap = pltpu.make_async_remote_copy(
        src_ref=ow_send,
        dst_ref=ow_all.at[:, swap_rows, swap_lanes],
        send_sem=swap_sem.at[0],
        recv_sem=swap_sem.at[1],
        device_id=swap_dev,
        device_id_type=MESH,
    )

    @pl.when(swap_here)
    def _():
        pltpu.make_async_copy(ow_send, ow_view(OWN_S, None), swap_sem.at[1]).start()

    @pl.when(jnp.logical_not(swap_here))
    def _():
        swap.start()

    rows_t[...] = jnp.zeros_like(rows_t)
    for s in range(3):
        for j in range(3):
            rows_t[3 * s + j : 3 * s + j + 1, :] = taps[s, j : j + 1, :]
    rows_t[9:10, :] = skip[...]
    taps_t[...] = rows_t[...].T

    local[2].wait()

    @pl.loop(0, ROWS // SUB)
    def _(b):
        v = acc[0, pl.ds(pl.multiple_of(b * SUB, SUB), SUB), :]
        fsend[pl.ds(pl.multiple_of(b * BLOCK, BLOCK), BLOCK), :] = v.reshape(BLOCK, SIDE).astype(BF16)

    def to_each(start):
        @pl.loop(0, CTX)
        def _(d):
            @pl.when(d != ctx)
            def _():
                start(d, True)

            @pl.when(d == ctx)
            def _():
                start(d, False)

    def filter_copy(d, remote):
        src = fsend.at[pl.ds(pl.multiple_of(d * 2 * BLOCK, 2 * BLOCK), 2 * BLOCK)]
        dst = frecv.at[ctx]
        if remote:
            return pltpu.make_async_remote_copy(
                src_ref=src, dst_ref=dst, send_sem=f_ss.at[d], recv_sem=f_rs.at[ctx],
                device_id=(d, tp), device_id_type=MESH,
            )
        return pltpu.make_async_copy(src, dst, f_rs.at[ctx])

    def part_copy(src_ref, dst_ref, ss, rs, h, d, remote):
        src, dst = src_ref.at[h, d], dst_ref.at[h, ctx]
        if remote:
            return pltpu.make_async_remote_copy(
                src_ref=src, dst_ref=dst, send_sem=ss.at[h, d], recv_sem=rs.at[h, ctx],
                device_id=(d, tp), device_id_type=MESH,
            )
        return pltpu.make_async_copy(src, dst, rs.at[h, ctx])

    w_g.recv("Bp")
    w_g.send("Dp")
    w_sib(LEFT)
    w_g.recv("Bm")
    w_g.send("Dm")
    w_sib(RIGHT)
    t_g.recv("Bp")
    t_g.send("Dp")
    t_g.recv("Bm")
    t_g.send("Dm")
    w_g.recv("A")
    w_g.send("Cp", "Cm")
    w_sib(PAIR_S)
    t_g.recv("A")
    t_g.send("Cp", "Cm")
    w_g.recv("Cp")
    w_g.send("Ep")
    w_sib(PLEFT)
    w_g.recv("Cm")
    w_g.send("Em")
    w_sib(PRIGHT)
    t_g.recv("Cp")
    t_g.send("Ep")
    t_g.recv("Cm")
    t_g.send("Em")
    to_each(lambda d, remote: filter_copy(d, remote).start())
    w_g.recv("Dp", "Dm")
    w_sib(FAR)
    w_g.recv("Ep", "Em")
    w_sib(PFAR)
    for shard in range(8):
        ref = w_view(shard, None, 1 - core)
        pltpu.make_async_copy(ref, ref, w_sib_rs.at[shard]).wait()
    local[3].wait()

    early, late = 6 * ROWS, 2 * ROWS

    @pl.loop(0, 12)
    def _(i):
        s, lanes = i // 4, pl.ds(pl.multiple_of((i % 4) * 256, 256), 256)
        acc[s, :, lanes] = dot(w_all[s, :, pl.ds(0, early)], tok_all[pl.ds(0, early), lanes])

    t_g.recv("Dp", "Dm", "Ep", "Em")

    def finish_tile(s, n):
        lanes = pl.ds(pl.multiple_of(n * 256, 256), 256)
        acc[s, :, lanes] = acc[s, :, lanes] + dot(
            w_all[s, :, pl.ds(early, late)], tok_all[pl.ds(early, late), lanes]
        )

    @pl.loop(0, 3)
    def _(s):
        finish_tile(s, 3)
        halo_send[s] = acc[s, :, pl.ds(SLAB - SIDE, SIDE)].T[SIDE - 8 :]

    halo = pltpu.make_async_remote_copy(
        src_ref=halo_send,
        dst_ref=halo_recv.at[:, pl.ds(SIDE - 8, 8)],
        send_sem=halo_sem.at[0],
        recv_sem=halo_sem.at[1],
        device_id=((ctx + 1) % CTX, tp),
        device_id_type=MESH,
    )
    halo.start()

    @pl.loop(0, 6)
    def _(i):
        finish_tile(1 + i // 3, i % 3)

    halo.wait_recv()
    for s in range(3):
        halo_t[s] = jnp.where(ctx > 0, halo_recv[s].T, 0.0)

    def short(s, r0):
        rows = pl.ds(r0, SUB)
        p = acc[s, rows, :]
        e = jnp.concatenate([halo_t[s, rows, :], p], axis=1)
        one = pltpu.roll(e, 1, 1)[:, SIDE:]
        two = pltpu.roll(e, 2, 1)[:, SIDE:]
        tap = taps_t[rows, :]
        return (
            tap[:, 3 * s : 3 * s + 1] * p
            + tap[:, 3 * s + 1 : 3 * s + 2] * one
            + tap[:, 3 * s + 2 : 3 * s + 3] * two
        )

    for h in range(PART):

        @pl.loop(0, CTX)
        def _(d):
            r0 = pl.multiple_of(d * OWN + h * SUB, SUB)
            g = (short(1, r0) * short(2, r0)).astype(BF16)
            gated[pl.ds(r0, SUB), :] = g
            gsend[h, d] = g.astype(F32).reshape(BLOCK, SIDE).astype(BF16)

            @pl.when(d != ctx)
            def _():
                part_copy(gsend, grecv, g_ss, g_rs, h, d, True).start()

            @pl.when(d == ctx)
            def _():
                part_copy(gsend, grecv, g_ss, g_rs, h, d, False).start()

    ow_g = Gather(ctx_devs, ow_view, lambda shard, there, half: ow_view(shard, half), ow_view, ow_ss, ow_rs)

    def ow_sib(shard):
        copy = sib_copy(ow_view, shard, ow_sib_ss, ow_sib_rs)
        copy.start()
        sib_sent.append(copy)

    ref = ow_view(OWN_S, None)
    pltpu.make_async_copy(ref, ref, swap_sem.at[1]).wait()
    ow_g.send("Bp", "Bm", "A")
    ow_sib(OWN_S)

    @pl.loop(0, 3)
    def _(n):
        finish_tile(0, n)

    @pl.loop(0, ROWS // SUB)
    def _(b):
        r0 = pl.multiple_of(b * SUB, SUB)
        acc[0, pl.ds(r0, SUB), :] = short(0, r0)

    def forward(c):
        pair = jnp.concatenate([xf[c].astype(BF16), xf[c + 1].astype(BF16)], axis=1)
        a = dot(f1[...], pair)
        cos, sin = tw[0], tw[1]
        turned = []
        for j in range(2):
            re, im = a[:SIDE, j * SIDE : (j + 1) * SIDE], a[SIDE:, j * SIDE : (j + 1) * SIDE]
            turned.append(jnp.concatenate([re * cos + im * sin, im * cos - re * sin], axis=1).astype(BF16))
        return dot(jnp.concatenate(turned, axis=0), f2[...])

    @pl.loop(0, CTX)
    def _(s):
        ref = frecv.at[s]
        pltpu.make_async_copy(ref, ref, f_rs.at[s]).wait()
        xf[:, pl.ds(pl.multiple_of(s * 8, 8), 8), :] = frecv[s].astype(F32).reshape(OWN, 8, SIDE)

    @pl.loop(0, OWN // 2)
    def _(i):
        spec[i] = forward(2 * i)

    def convolve(h):
        part = pl.ds(h * SUB, SUB)

        @pl.loop(0, CTX)
        def _(s):
            ref = grecv.at[h, s]
            pltpu.make_async_copy(ref, ref, g_rs.at[h, s]).wait()
            xf[part, pl.ds(pl.multiple_of(s * 8, 8), 8), :] = grecv[h, s].astype(F32).reshape(SUB, 8, SIDE)

        @pl.loop(0, SUB // 2)
        def _(i):
            c = h * SUB + 2 * i
            x_f, h_f = forward(c), spec[h * (SUB // 2) + i]
            xr, xi, hr, hi = x_f[:, :SIDE], x_f[:, SIDE:], h_f[:, :SIDE], h_f[:, SIDE:]
            prod = jnp.concatenate([xr * hr - xi * hi, xr * hi + xi * hr], axis=1).astype(BF16)
            b = dot(prod, f3[...])
            cos, sin = tw[0], tw[1]
            back = []
            for j in range(2):
                re, im = b[j * SIDE : (j + 1) * SIDE, :SIDE], b[j * SIDE : (j + 1) * SIDE, SIDE:]
                back.append(jnp.concatenate([re * cos - im * sin, im * cos + re * sin], axis=0).astype(BF16))
            y = dot(f4[...], jnp.concatenate(back, axis=1))
            xf[c] = y[:, :SIDE]
            xf[c + 1] = y[:, SIDE:]

        @pl.loop(0, CTX)
        def _(d):
            v = xf[part, pl.ds(pl.multiple_of(d * 8, 8), 8), :]
            lsend[h, d] = v.reshape(BLOCK, SIDE).astype(BF16)

            @pl.when(d != ctx)
            def _():
                part_copy(lsend, lrecv, l_ss, l_rs, h, d, True).start()

            @pl.when(d == ctx)
            def _():
                part_copy(lsend, lrecv, l_ss, l_rs, h, d, False).start()

    def hid_view(h):
        def view(shard, half):
            if half is None:
                return hid_all.at[h, pl.ds(shard * HALF, HALF)]
            return hid_all.at[h, pl.ds(shard * HALF + half * (HALF // 2), HALF // 2)]

        return view

    h_g = [
        Gather(
            tp_devs, hid_view(h), lambda shard, there, half, h=h: hid_view(h)(there, half), hid_view(h),
            h_ss.at[h], h_rs.at[h],
        )
        for h in range(PART)
    ]

    def hidden(h):
        @pl.loop(0, CTX)
        def _(d):
            ref = lrecv.at[h, d]
            pltpu.make_async_copy(ref, ref, l_rs.at[h, d]).wait()
            rows = pl.ds(pl.multiple_of(d * OWN + h * SUB, SUB), SUB)
            long_rows = lrecv[h, d].astype(F32).reshape(SUB, SLAB)
            gain = taps_t[rows, :][:, 9:10]
            v = (long_rows + gain * gated[rows, :].astype(F32)) * acc[0, rows, :]
            hid_all[h, pl.ds(pl.multiple_of(d * SUB, SUB), SUB), :] = v.astype(BF16)

    convolve(0)
    ow_g.recv("Bp")
    ow_g.send("Dp")
    ow_sib(LEFT)
    ow_g.recv("Bm")
    ow_g.send("Dm")
    ow_sib(RIGHT)
    ow_g.recv("A")
    ow_g.send("Cp", "Cm")
    ow_sib(PAIR_S)
    convolve(1)
    hidden(0)
    h_g[0].send("Bp", "Bm", "A")
    ow_g.recv("Cp")
    ow_g.send("Ep")
    ow_sib(PLEFT)
    ow_g.recv("Cm")
    ow_g.send("Em")
    ow_sib(PRIGHT)
    hidden(1)
    h_g[1].send("Bp", "Bm", "A")
    ow_g.recv("Dp", "Dm")
    ow_sib(FAR)
    ow_g.recv("Ep", "Em")
    ow_sib(PFAR)
    h_g[0].recv("Bp")
    h_g[0].send("Dp")
    h_g[0].recv("Bm")
    h_g[0].send("Dm")
    h_g[0].recv("A")
    h_g[0].send("Cp", "Cm")
    h_g[1].recv("Bp")
    h_g[1].send("Dp", "AL")
    h_g[1].recv("Bm")
    h_g[1].send("Dm", "AR")
    h_g[0].recv("Cp")
    h_g[0].send("Ep")
    h_g[0].recv("Cm")
    h_g[0].send("Em")
    h_g[1].recv("Dp")
    h_g[1].send("AF0")
    h_g[1].recv("Dm")
    h_g[1].send("AF1")
    for shard in range(8):
        ref = ow_view(shard, None, 1 - core)
        pltpu.make_async_copy(ref, ref, ow_sib_rs.at[shard]).wait()

    def outward(h, k0, k1, first, last):
        @pl.loop(0, 4)
        def _(n):
            lanes = pl.ds(pl.multiple_of(n * 256, 256), 256)
            v = dot(ow_all[h, :, pl.ds(k0, k1 - k0)], hid_all[h, pl.ds(k0, k1 - k0), lanes])
            if not first:
                v = v + acc[1, :, lanes]
            if last:
                out[:, lanes] = v.astype(BF16)
            else:
                acc[1, :, lanes] = v

    outward(0, 0, 6 * HALF, True, False)
    h_g[0].recv("Dp", "Dm", "Ep", "Em")
    outward(0, 6 * HALF, 8 * HALF, False, False)
    h_g[1].recv("A", "AL", "AR")
    outward(1, 0, 6 * HALF, False, False)
    h_g[1].recv("AF0", "AF1")
    outward(1, 6 * HALF, 8 * HALF, False, True)

    for gather in (t_g, w_g, ow_g, *h_g):
        gather.finish()
    for copy in sib_sent:
        copy.wait_send()

    @pl.when(jnp.logical_not(swap_here))
    def _():
        swap.wait_send()

    halo.wait_send()

    @pl.loop(0, CTX)
    def _(d):
        @pl.when(d != ctx)
        def _():
            filter_copy(d, True).wait_send()
            for h in range(PART):
                part_copy(gsend, grecv, g_ss, g_rs, h, d, True).wait_send()
                part_copy(lsend, lrecv, l_ss, l_rs, h, d, True).wait_send()


def per_device(tokens, in_weight, short_taps, long_filter, skip_gain, out_weight):
    hbm = pl.BlockSpec(memory_space=pl.ANY)
    vmem = pl.BlockSpec(memory_space=pltpu.VMEM)
    dma = pltpu.SemaphoreType.DMA
    return pl.pallas_call(
        kernel,
        out_shape=jax.ShapeDtypeStruct((ROWS, SLAB), BF16),
        in_specs=[hbm, hbm, vmem, hbm, vmem, hbm, vmem, vmem, vmem, vmem, vmem],
        out_specs=vmem,
        scratch_shapes=[
            pltpu.VMEM((TP * ROWS, SLAB), BF16),
            pltpu.VMEM((3, ROWS, TP * ROWS), BF16),
            pltpu.VMEM((PART, ROWS, TP * HALF), BF16),
            pltpu.VMEM((PART, TP * HALF, SLAB), BF16),
            pltpu.VMEM((3, ROWS, SLAB), F32),
            pltpu.VMEM((3, WROWS, ROWS), BF16),
            pltpu.VMEM((ROWS, WROWS), BF16),
            pltpu.VMEM((PART, WROWS, HALF), BF16),
            pltpu.VMEM((ROWS * 8, SIDE), BF16),
            pltpu.VMEM((CTX, 2 * BLOCK, SIDE), BF16),
            pltpu.VMEM((ROWS, SLAB), BF16),
            pltpu.VMEM((PART, CTX, BLOCK, SIDE), BF16),
            pltpu.VMEM((PART, CTX, BLOCK, SIDE), BF16),
            pltpu.VMEM((OWN, SIDE, SIDE), F32),
            pltpu.VMEM((OWN // 2, 2 * SIDE, 2 * SIDE), F32),
            pltpu.VMEM((PART, CTX, BLOCK, SIDE), BF16),
            pltpu.VMEM((PART, CTX, BLOCK, SIDE), BF16),
            pltpu.VMEM((3, 8, ROWS), F32),
            pltpu.VMEM((3, SIDE, ROWS), F32),
            pltpu.VMEM((3, ROWS, SIDE), F32),
            pltpu.VMEM((SIDE, ROWS), F32),
            pltpu.VMEM((ROWS, SIDE), F32),
            dma((4,)),
            dma((9,)), dma((9,)),
            dma((9,)), dma((9,)),
            dma((9,)), dma((9,)),
            dma((PART, 9)), dma((PART, 9)),
            dma((8,)), dma((8,)),
            dma((8,)), dma((8,)),
            dma((2,)),
            dma((2,)),
            dma((CTX,)), dma((CTX,)),
            dma((PART, CTX)), dma((PART, CTX)),
            dma((PART, CTX)), dma((PART, CTX)),
        ],
        compiler_params=pltpu.CompilerParams(
            collective_id=0, has_side_effects=True, vmem_limit_bytes=62 * 2**20
        ),
        cost_estimate=pl.CostEstimate(
            flops=2 * (3 * ROWS * TP * ROWS * SLAB + TP * ROWS * ROWS * SLAB) + 2_400_000_000,
            bytes_accessed=8 * 2**20,
            transcendentals=0,
        ),
        name="hyena",
    )(
        tokens,
        in_weight,
        jnp.swapaxes(short_taps, 1, 2),
        long_filter,
        skip_gain.reshape(1, ROWS),
        out_weight,
        *tables(),
    )


def solution(mesh):
    placed = (
        P("tp", "ctx"),
        P(None, "ctx", "tp"),
        P(None, "tp", None),
        P("tp", "ctx"),
        P("tp"),
        P("tp", "ctx"),
    )
    return jax.shard_map(
        per_device, mesh=mesh, in_specs=placed, out_specs=P("tp", "ctx"), check_vma=False
    )
```

```python
import functools
import math

import jax
import jax.numpy as jnp
import numpy as np
from jax import lax
from jax.experimental import pallas as pl
from jax.experimental.pallas import tpu as pltpu
from jax.sharding import PartitionSpec as P

MESH = pl.DeviceIdType.MESH
BF16 = jnp.bfloat16
F32 = jnp.float32

RING = 4
PAIR = 2
CTX = 16
TP = 8
ROWS = 512
SLAB = 1024
WROWS = 256
OWN = 32
SIDE = 128
PART = 2
SUB = OWN // PART
HALF = ROWS // PART
PIECES = ((0, 0, HALF), (1, 0, 64), (1, 64, HALF - 64))
BLOCK = SUB * 8

OWN_S, PAIR_S, LEFT, RIGHT, PLEFT, PRIGHT, FAR, PFAR = range(8)
COPIES = {
    "A": (0, OWN_S, PAIR_S, None, "pair"),
    "Bp": (1, OWN_S, LEFT, None, "plus"),
    "Bm": (2, OWN_S, RIGHT, None, "minus"),
    "Cp": (3, PAIR_S, PLEFT, None, "plus"),
    "Cm": (4, PAIR_S, PRIGHT, None, "minus"),
    "Dp": (5, LEFT, FAR, 0, "plus"),
    "Dm": (6, RIGHT, FAR, 1, "minus"),
    "Ep": (7, PLEFT, PFAR, 0, "plus"),
    "Em": (8, PRIGHT, PFAR, 1, "minus"),
    "AL": (3, LEFT, PLEFT, None, "pair"),
    "AR": (4, RIGHT, PRIGHT, None, "pair"),
    "AF0": (7, FAR, PFAR, 0, "pair"),
    "AF1": (8, FAR, PFAR, 1, "pair"),
}


def tables():
    i = np.arange(SIDE)
    quarter = 2 * np.pi * ((i[:, None] * (4 * i[None, :] + 1)) % (4 * SIDE)) / (4 * SIDE)
    plain = 2 * np.pi * ((i[:, None] * i[None, :]) % SIDE) / SIDE
    twist = 2 * np.pi * (((4 * i[:, None] + 1) * i[None, :]) % (4 * SIDE * SIDE)) / (4 * SIDE * SIDE)
    f1 = np.concatenate([np.cos(quarter.T), -np.sin(quarter.T)], 0)
    c, s = np.cos(plain), np.sin(plain)
    f2 = np.block([[c, -s], [s, c]])
    f3 = np.block([[c, s], [-s, c]])
    f4 = np.concatenate([np.cos(quarter), -np.sin(quarter)], 1) / (SIDE * SIDE)
    tw = np.stack([np.cos(twist), np.sin(twist)])
    return [jnp.asarray(a, BF16) for a in (f1, f2, f3, f4)] + [jnp.asarray(tw, F32)]


def rel_slot(dring, dpair):
    return 3 * dring - 7 * (dring // 3) + dpair * (1 + dring % 2)


class Gather:
    def __init__(self, devs, src, dst, got, send_sem, recv_sem):
        self.devs, self.src, self.dst, self.got = devs, src, dst, got
        self.send_sem, self.recv_sem = send_sem, recv_sem
        self.sent = []

    def send(self, *names):
        for name in names:
            i, shard, there, half, to = COPIES[name]
            copy = pltpu.make_async_remote_copy(
                src_ref=self.src(shard, half),
                dst_ref=self.dst(shard, there, half),
                send_sem=self.send_sem.at[i],
                recv_sem=self.recv_sem.at[i],
                device_id=self.devs[to],
                device_id_type=MESH,
            )
            copy.start()
            self.sent.append(copy)

    def recv(self, *names):
        for name in names:
            i, _, there, half, to = COPIES[name]
            ref = self.got(there, half)
            pltpu.make_async_copy(ref, ref, self.recv_sem.at[i]).wait()

    def finish(self):
        for copy in self.sent:
            copy.wait_send()


def dot(a, b):
    return jnp.dot(a, b, preferred_element_type=F32)


def kernel(
    tok, w, taps, filt, skip, ow, f1, f2, f3, f4, tw,
    out,
    tok_all, w_all, ow_all, hid_all, acc, w_st, ow_st, ow_send, ow_held,
    fsend, frecv, gated, gsend, grecv, xf, spec, lsend, lrecv,
    halo_send, halo_recv, halo_t, rows_t, taps_t,
    local_sem, tok_ss, tok_rs, w_ss, w_rs, ow_ss, ow_rs, h_ss, h_rs, w_sib_ss, w_sib_rs, ow_sib_ss, ow_sib_rs,
    swap_sem, halo_sem, f_ss, f_rs, g_ss, g_rs, l_ss, l_rs,
):
    ctx, tp = lax.axis_index("ctx"), lax.axis_index("tp")
    y_lo, z, core = ctx // 8, (ctx // 2) % 4, ctx % 2
    y_hi, x = tp // 4, tp % 4

    def ctx_at(y, zz, c):
        return y * 8 + zz * 2 + c

    tp_devs = {
        "pair": (ctx, (1 - y_hi) * 4 + x),
        "plus": (ctx, y_hi * 4 + (x + 1) % 4),
        "minus": (ctx, y_hi * 4 + (x + 3) % 4),
    }
    ctx_devs = {
        "pair": (ctx_at(1 - y_lo, z, core), tp),
        "plus": (ctx_at(y_lo, (z + 1) % 4, core), tp),
        "minus": (ctx_at(y_lo, (z + 3) % 4, core), tp),
    }
    sibling = (ctx_at(y_lo, z, 1 - core), tp)
    cross_dev = (ctx_at(y_hi, z, core), y_lo * 4 + x)
    cross_away = y_hi != y_lo
    swap_dev = (ctx_at(y_lo, x, core), y_hi * 4 + z)
    swap_away = x != z

    local = [
        pltpu.make_async_copy(w, w_st, local_sem.at[0]),
        pltpu.make_async_copy(ow, ow_st, local_sem.at[1]),
        pltpu.make_async_copy(filt, acc.at[0], local_sem.at[2]),
        pltpu.make_async_copy(tok, tok_all.at[pl.ds(0, ROWS)], local_sem.at[3]),
    ]
    for copy in local:
        copy.start()
    halo_recv[...] = jnp.zeros_like(halo_recv)

    barrier = pltpu.get_barrier_semaphore()
    for i in range(1, CTX):
        pl.semaphore_signal(barrier, inc=1, device_id=((ctx + i) % CTX, tp), device_id_type=MESH)
    for d in tp_devs.values():
        pl.semaphore_signal(barrier, inc=1, device_id=d, device_id_type=MESH)

    @pl.when(cross_away)
    def _():
        pl.semaphore_signal(barrier, inc=1, device_id=cross_dev, device_id_type=MESH)

    @pl.when(swap_away)
    def _():
        pl.semaphore_signal(barrier, inc=1, device_id=swap_dev, device_id_type=MESH)

    pl.semaphore_wait(barrier, CTX - 1 + 3 + cross_away.astype(jnp.int32) + swap_away.astype(jnp.int32))

    def tok_gather(k):
        def rows(shard, half):
            if half is None:
                return pl.ds(shard * ROWS + k * HALF, HALF)
            return pl.ds(shard * ROWS + k * HALF + half * (HALF // 2), HALF // 2)

        def src(shard, half):
            return (tok if shard == OWN_S else tok_all).at[rows(shard, half)]

        return Gather(
            tp_devs, src, lambda shard, there, half: tok_all.at[rows(there, half)],
            lambda there, half: tok_all.at[rows(there, half)], tok_ss.at[k], tok_rs.at[k],
        )

    t_g = [tok_gather(k) for k in range(2)]
    t_g[0].send("Bp", "Bm")

    def w_slot(shard):
        dz = {OWN_S: 0, PAIR_S: 0, LEFT: 3, RIGHT: 1, PLEFT: 3, PRIGHT: 1, FAR: 2, PFAR: 2}[shard]
        dy = 1 if shard in (PAIR_S, PLEFT, PRIGHT, PFAR) else 0
        return rel_slot((z + dz + 4 - x) % 4, (y_lo + dy + y_hi) % 2)

    def w_lanes(shard, c):
        return pl.ds(pl.multiple_of(w_slot(shard) * ROWS + c * WROWS, WROWS), WROWS)

    def w_view(shard, half, c=core):
        return w_all.at[:, :, w_lanes(shard, c)]

    def w_gather(k):
        def view(shard, half):
            if half is None:
                return w_all.at[:, pl.ds(k * HALF, HALF), w_lanes(shard, core)]
            return w_all.at[:, pl.ds(k * HALF + half * (HALF // 2), HALF // 2), w_lanes(shard, core)]

        return Gather(ctx_devs, view, lambda shard, there, half: view(shard, half), view, w_ss.at[k], w_rs.at[k])

    w_g = [w_gather(k) for k in range(2)]

    def sib_copy(view, shard, ss, rs):
        return pltpu.make_async_remote_copy(
            src_ref=view(shard, None),
            dst_ref=view(shard, None),
            send_sem=ss.at[shard],
            recv_sem=rs.at[shard],
            device_id=sibling,
            device_id_type=MESH,
        )

    sib_sent = []

    def w_sib(shard):
        copy = sib_copy(w_view, shard, w_sib_ss, w_sib_rs)
        copy.start()
        sib_sent.append(copy)

    local[0].wait()
    for s in range(3):
        w_all[s, :, w_lanes(OWN_S, core)] = w_st[s].T
    w_g[0].send("A", "Bp", "Bm")
    w_g[1].send("A")
    w_sib(OWN_S)

    def ow_view(shard, half, c=core):
        lanes = pl.ds(pl.multiple_of(w_slot(shard) * HALF, HALF), HALF)
        rows = pl.ds(pl.multiple_of(c * WROWS, WROWS), WROWS)
        if half is None:
            return ow_all.at[:, rows, lanes]
        return ow_all.at[half, rows, lanes]

    local[1].wait()
    for h in range(PART):
        picked = jnp.concatenate([ow_st[pl.ds(d * OWN + h * SUB, SUB), :] for d in range(CTX)], axis=0)
        ow_send[h] = picked.T
    cross = pltpu.make_async_remote_copy(
        src_ref=ow_send,
        dst_ref=ow_held,
        send_sem=swap_sem.at[0],
        recv_sem=swap_sem.at[1],
        device_id=cross_dev,
        device_id_type=MESH,
    )

    swap_lanes = pl.ds(pl.multiple_of(rel_slot((x + 4 - z) % 4, (y_hi + y_lo) % 2) * HALF, HALF), HALF)
    swap_rows = pl.ds(pl.multiple_of(core * WROWS, WROWS), WROWS)
    swap = pltpu.make_async_remote_copy(
        src_ref=ow_held,
        dst_ref=ow_all.at[:, swap_rows, swap_lanes],
        send_sem=swap_sem.at[2],
        recv_sem=swap_sem.at[3],
        device_id=swap_dev,
        device_id_type=MESH,
    )

    rows_t[...] = jnp.zeros_like(rows_t)
    for s in range(3):
        for j in range(3):
            rows_t[3 * s + j : 3 * s + j + 1, :] = taps[s, j : j + 1, :]
    rows_t[9:10, :] = skip[...]
    taps_t[...] = rows_t[...].T

    local[2].wait()

    @pl.loop(0, ROWS // SUB)
    def _(b):
        v = acc[0, pl.ds(pl.multiple_of(b * SUB, SUB), SUB), :]
        fsend[pl.ds(pl.multiple_of(b * BLOCK, BLOCK), BLOCK), :] = v.reshape(BLOCK, SIDE).astype(BF16)

    def to_each(start):
        @pl.loop(0, CTX)
        def _(d):
            @pl.when(d != ctx)
            def _():
                start(d, True)

            @pl.when(d == ctx)
            def _():
                start(d, False)

    def filter_copy(d, remote):
        src = fsend.at[pl.ds(pl.multiple_of(d * 2 * BLOCK, 2 * BLOCK), 2 * BLOCK)]
        dst = frecv.at[ctx]
        if remote:
            return pltpu.make_async_remote_copy(
                src_ref=src, dst_ref=dst, send_sem=f_ss.at[d], recv_sem=f_rs.at[ctx],
                device_id=(d, tp), device_id_type=MESH,
            )
        return pltpu.make_async_copy(src, dst, f_rs.at[ctx])

    def part_copy(src_ref, dst_ref, ss, rs, h, d, remote):
        src, dst = src_ref.at[h, d], dst_ref.at[h, ctx]
        if remote:
            return pltpu.make_async_remote_copy(
                src_ref=src, dst_ref=dst, send_sem=ss.at[h, d], recv_sem=rs.at[h, ctx],
                device_id=(d, tp), device_id_type=MESH,
            )
        return pltpu.make_async_copy(src, dst, rs.at[h, ctx])

    w_g[0].recv("Bp", "Bm")
    w_g[1].send("Bp", "Bm")
    w_g[0].send("Dp", "Dm")
    t_g[0].send("A")
    t_g[1].send("Bp", "Bm")
    t_g[0].recv("Bp", "Bm")
    t_g[0].send("Dp", "Dm")
    t_g[1].send("A")
    w_g[1].recv("Bp", "Bm")
    w_g[1].send("Dp", "Dm")
    w_sib(LEFT)
    w_sib(RIGHT)
    w_g[0].recv("A")
    w_g[0].send("Cp", "Cm")
    w_g[1].recv("A")
    w_g[1].send("Cp", "Cm")
    w_sib(PAIR_S)
    t_g[0].recv("A")
    t_g[0].send("Cp", "Cm")
    t_g[1].recv("Bp", "Bm")
    t_g[1].send("Dp", "Dm")
    w_g[0].recv("Cp", "Cm")
    w_g[0].send("Ep", "Em")
    t_g[1].recv("A")
    t_g[1].send("Cp", "Cm")

    @pl.when(cross_away)
    def _():
        cross.start()

    @pl.when(jnp.logical_not(cross_away))
    def _():
        pltpu.make_async_copy(ow_send, ow_held, swap_sem.at[1]).start()

    w_g[1].recv("Cp", "Cm")
    w_g[1].send("Ep", "Em")
    w_sib(PLEFT)
    w_sib(PRIGHT)
    for g in w_g:
        g.recv("Dp", "Dm")
    w_sib(FAR)
    t_g[0].recv("Cp", "Cm")
    t_g[0].send("Ep", "Em")
    for g in w_g:
        g.recv("Ep", "Em")
    w_sib(PFAR)
    to_each(lambda d, remote: filter_copy(d, remote).start())
    t_g[1].recv("Cp", "Cm")
    t_g[1].send("Ep", "Em")
    for shard in range(8):
        ref = w_view(shard, None, 1 - core)
        pltpu.make_async_copy(ref, ref, w_sib_rs.at[shard]).wait()
    local[3].wait()

    early, late = 6 * ROWS, 2 * ROWS

    @pl.loop(0, 12)
    def _(i):
        s, lanes = i // 4, pl.ds(pl.multiple_of((i % 4) * 256, 256), 256)
        acc[s, :, lanes] = dot(w_all[s, :, pl.ds(0, early)], tok_all[pl.ds(0, early), lanes])

    def forward(c):
        pair = jnp.concatenate([xf[c].astype(BF16), xf[c + 1].astype(BF16)], axis=1)
        a = dot(f1[...], pair)
        cos, sin = tw[0], tw[1]
        turned = []
        for j in range(2):
            re, im = a[:SIDE, j * SIDE : (j + 1) * SIDE], a[SIDE:, j * SIDE : (j + 1) * SIDE]
            turned.append(jnp.concatenate([re * cos + im * sin, im * cos - re * sin], axis=1).astype(BF16))
        return dot(jnp.concatenate(turned, axis=0), f2[...])

    @pl.loop(0, CTX)
    def _(s):
        ref = frecv.at[s]
        pltpu.make_async_copy(ref, ref, f_rs.at[s]).wait()
        xf[:, pl.ds(pl.multiple_of(s * 8, 8), 8), :] = frecv[s].astype(F32).reshape(OWN, 8, SIDE)

    @pl.loop(0, OWN // 2, unroll=4)
    def _(i):
        spec[i] = forward(2 * i)

    for g in t_g:
        g.recv("Dp", "Dm", "Ep", "Em")

    pltpu.make_async_copy(ow_held, ow_held, swap_sem.at[1]).wait()

    @pl.when(swap_away)
    def _():
        swap.start()

    @pl.when(jnp.logical_not(swap_away))
    def _():
        pltpu.make_async_copy(ow_held, ow_view(OWN_S, None), swap_sem.at[3]).start()

    def finish_tile(s, n):
        lanes = pl.ds(pl.multiple_of(n * 256, 256), 256)
        acc[s, :, lanes] = acc[s, :, lanes] + dot(
            w_all[s, :, pl.ds(early, late)], tok_all[pl.ds(early, late), lanes]
        )

    @pl.loop(0, 3)
    def _(s):
        finish_tile(s, 3)
        halo_send[s] = acc[s, :, pl.ds(SLAB - SIDE, SIDE)].T[SIDE - 8 :]

    halo = pltpu.make_async_remote_copy(
        src_ref=halo_send,
        dst_ref=halo_recv.at[:, pl.ds(SIDE - 8, 8)],
        send_sem=halo_sem.at[0],
        recv_sem=halo_sem.at[1],
        device_id=((ctx + 1) % CTX, tp),
        device_id_type=MESH,
    )
    halo.start()

    @pl.loop(0, 6)
    def _(i):
        finish_tile(1 + i // 3, i % 3)

    halo.wait_recv()
    for s in range(3):
        halo_t[s] = jnp.where(ctx > 0, halo_recv[s].T, 0.0)

    def short(s, r0):
        rows = pl.ds(r0, SUB)
        p = acc[s, rows, :]
        e = jnp.concatenate([halo_t[s, rows, :], p], axis=1)
        one = pltpu.roll(e, 1, 1)[:, SIDE:]
        two = pltpu.roll(e, 2, 1)[:, SIDE:]
        tap = taps_t[rows, :]
        return (
            tap[:, 3 * s : 3 * s + 1] * p
            + tap[:, 3 * s + 1 : 3 * s + 2] * one
            + tap[:, 3 * s + 2 : 3 * s + 3] * two
        )

    for h in range(PART):

        @pl.loop(0, CTX)
        def _(d):
            r0 = pl.multiple_of(d * OWN + h * SUB, SUB)
            g = (short(1, r0) * short(2, r0)).astype(BF16)
            gated[pl.ds(r0, SUB), :] = g
            gsend[h, d] = g.astype(F32).reshape(BLOCK, SIDE).astype(BF16)

            @pl.when(d != ctx)
            def _():
                part_copy(gsend, grecv, g_ss, g_rs, h, d, True).start()

            @pl.when(d == ctx)
            def _():
                part_copy(gsend, grecv, g_ss, g_rs, h, d, False).start()

    ow_g = Gather(ctx_devs, ow_view, lambda shard, there, half: ow_view(shard, half), ow_view, ow_ss, ow_rs)

    def ow_sib(shard):
        copy = sib_copy(ow_view, shard, ow_sib_ss, ow_sib_rs)
        copy.start()
        sib_sent.append(copy)

    @pl.loop(0, 3)
    def _(n):
        finish_tile(0, n)

    @pl.loop(0, ROWS // SUB)
    def _(b):
        r0 = pl.multiple_of(b * SUB, SUB)
        acc[0, pl.ds(r0, SUB), :] = short(0, r0)

    def take(h):
        part = pl.ds(h * SUB, SUB)

        @pl.loop(0, CTX)
        def _(s):
            ref = grecv.at[h, s]
            pltpu.make_async_copy(ref, ref, g_rs.at[h, s]).wait()
            xf[part, pl.ds(pl.multiple_of(s * 8, 8), 8), :] = grecv[h, s].astype(F32).reshape(SUB, 8, SIDE)

    def convolve(h):
        part = pl.ds(h * SUB, SUB)

        @pl.loop(0, SUB // 2, unroll=4)
        def _(i):
            c = h * SUB + 2 * i
            x_f, h_f = forward(c), spec[h * (SUB // 2) + i]
            xr, xi, hr, hi = x_f[:, :SIDE], x_f[:, SIDE:], h_f[:, :SIDE], h_f[:, SIDE:]
            prod = jnp.concatenate([xr * hr - xi * hi, xr * hi + xi * hr], axis=1).astype(BF16)
            b = dot(prod, f3[...])
            cos, sin = tw[0], tw[1]
            back = []
            for j in range(2):
                re, im = b[j * SIDE : (j + 1) * SIDE, :SIDE], b[j * SIDE : (j + 1) * SIDE, SIDE:]
                back.append(jnp.concatenate([re * cos - im * sin, im * cos + re * sin], axis=0).astype(BF16))
            y = dot(f4[...], jnp.concatenate(back, axis=1))
            xf[c] = y[:, :SIDE]
            xf[c + 1] = y[:, SIDE:]

        @pl.loop(0, CTX)
        def _(d):
            v = xf[part, pl.ds(pl.multiple_of(d * 8, 8), 8), :]
            lsend[h, d] = v.reshape(BLOCK, SIDE).astype(BF16)

            @pl.when(d != ctx)
            def _():
                part_copy(lsend, lrecv, l_ss, l_rs, h, d, True).start()

            @pl.when(d == ctx)
            def _():
                part_copy(lsend, lrecv, l_ss, l_rs, h, d, False).start()

    def hid_gather(i):
        h, first, count = PIECES[i]

        def view(shard, half):
            if half is None:
                return hid_all.at[h, pl.ds(shard * HALF + first, count)]
            return hid_all.at[h, pl.ds(shard * HALF + first + half * (count // 2), count // 2)]

        return Gather(
            tp_devs, view, lambda shard, there, half: view(there, half), view, h_ss.at[i], h_rs.at[i]
        )

    h_g = [hid_gather(i) for i in range(len(PIECES))]

    def hidden(h):
        @pl.loop(0, CTX)
        def _(d):
            ref = lrecv.at[h, d]
            pltpu.make_async_copy(ref, ref, l_rs.at[h, d]).wait()
            rows = pl.ds(pl.multiple_of(d * OWN + h * SUB, SUB), SUB)
            long_rows = lrecv[h, d].astype(F32).reshape(SUB, SLAB)
            gain = taps_t[rows, :][:, 9:10]
            v = (long_rows + gain * gated[rows, :].astype(F32)) * acc[0, rows, :]
            hid_all[h, pl.ds(pl.multiple_of(d * SUB, SUB), SUB), :] = v.astype(BF16)

    take(0)
    convolve(0)
    ref = ow_view(OWN_S, None)
    pltpu.make_async_copy(ref, ref, swap_sem.at[3]).wait()
    take(1)
    ow_g.send("A", "Bp", "Bm")
    ow_sib(OWN_S)
    convolve(1)
    hidden(0)
    h_g[0].send("A", "Bp", "Bm")
    ow_g.recv("Bp", "Bm")
    ow_g.send("Dp", "Dm")
    ow_sib(LEFT)
    ow_sib(RIGHT)
    ow_g.recv("A")
    ow_g.send("Cp", "Cm")
    ow_sib(PAIR_S)
    hidden(1)
    h_g[2].send("Bp", "Bm", "A")
    h_g[1].send("A", "Bp", "Bm")
    ow_g.recv("Cp", "Cm")
    ow_g.send("Ep", "Em")
    ow_sib(PLEFT)
    ow_sib(PRIGHT)
    h_g[0].recv("Bp", "Bm")
    h_g[0].send("Dp", "Dm")
    h_g[0].recv("A")
    h_g[0].send("Cp", "Cm")
    ow_g.recv("Dp", "Dm")
    ow_sib(FAR)
    ow_g.recv("Ep", "Em")
    ow_sib(PFAR)
    h_g[2].recv("Bp")
    h_g[2].send("Dp", "AL")
    h_g[2].recv("Bm")
    h_g[2].send("Dm", "AR")
    h_g[1].recv("Bp", "Bm")
    h_g[1].send("Dp", "Dm")
    h_g[1].recv("A")
    h_g[1].send("Cp", "Cm")
    h_g[0].recv("Cp", "Cm")
    h_g[0].send("Ep", "Em")
    h_g[2].recv("Dp")
    h_g[2].send("AF0")
    h_g[2].recv("Dm")
    h_g[2].send("AF1")
    h_g[1].recv("Cp", "Cm")
    h_g[1].send("Ep", "Em")
    for shard in range(8):
        ref = ow_view(shard, None, 1 - core)
        pltpu.make_async_copy(ref, ref, ow_sib_rs.at[shard]).wait()

    def outward(h, k0, k1, first, last):
        @pl.loop(0, 4)
        def _(n):
            lanes = pl.ds(pl.multiple_of(n * 256, 256), 256)
            v = dot(ow_all[h, :, pl.ds(k0, k1 - k0)], hid_all[h, pl.ds(k0, k1 - k0), lanes])
            if not first:
                v = v + acc[1, :, lanes]
            if last:
                out[:, lanes] = v.astype(BF16)
            else:
                acc[1, :, lanes] = v

    outward(0, 0, 6 * HALF, True, False)
    h_g[0].recv("Dp", "Dm", "Ep", "Em")
    outward(0, 6 * HALF, 8 * HALF, False, False)
    h_g[2].recv("A", "AL", "AR")
    outward(1, 0, 6 * HALF, False, False)
    h_g[1].recv("Dp", "Dm", "Ep", "Em")
    h_g[2].recv("AF0", "AF1")
    outward(1, 6 * HALF, 8 * HALF, False, True)

    for gather in (*t_g, *w_g, ow_g, *h_g):
        gather.finish()
    for copy in sib_sent:
        copy.wait_send()

    @pl.when(cross_away)
    def _():
        cross.wait_send()

    @pl.when(swap_away)
    def _():
        swap.wait_send()

    halo.wait_send()

    @pl.loop(0, CTX)
    def _(d):
        @pl.when(d != ctx)
        def _():
            filter_copy(d, True).wait_send()
            for h in range(PART):
                part_copy(gsend, grecv, g_ss, g_rs, h, d, True).wait_send()
                part_copy(lsend, lrecv, l_ss, l_rs, h, d, True).wait_send()


def per_device(tokens, in_weight, short_taps, long_filter, skip_gain, out_weight):
    hbm = pl.BlockSpec(memory_space=pl.ANY)
    vmem = pl.BlockSpec(memory_space=pltpu.VMEM)
    dma = pltpu.SemaphoreType.DMA
    return pl.pallas_call(
        kernel,
        out_shape=jax.ShapeDtypeStruct((ROWS, SLAB), BF16),
        in_specs=[hbm, hbm, vmem, hbm, vmem, hbm, vmem, vmem, vmem, vmem, vmem],
        out_specs=vmem,
        scratch_shapes=[
            pltpu.VMEM((TP * ROWS, SLAB), BF16),
            pltpu.VMEM((3, ROWS, TP * ROWS), BF16),
            pltpu.VMEM((PART, ROWS, TP * HALF), BF16),
            pltpu.VMEM((PART, TP * HALF, SLAB), BF16),
            pltpu.VMEM((3, ROWS, SLAB), F32),
            pltpu.VMEM((3, WROWS, ROWS), BF16),
            pltpu.VMEM((ROWS, WROWS), BF16),
            pltpu.VMEM((PART, WROWS, HALF), BF16),
            pltpu.VMEM((PART, WROWS, HALF), BF16),
            pltpu.VMEM((ROWS * 8, SIDE), BF16),
            pltpu.VMEM((CTX, 2 * BLOCK, SIDE), BF16),
            pltpu.VMEM((ROWS, SLAB), BF16),
            pltpu.VMEM((PART, CTX, BLOCK, SIDE), BF16),
            pltpu.VMEM((PART, CTX, BLOCK, SIDE), BF16),
            pltpu.VMEM((OWN, SIDE, SIDE), F32),
            pltpu.VMEM((OWN // 2, 2 * SIDE, 2 * SIDE), F32),
            pltpu.VMEM((PART, CTX, BLOCK, SIDE), BF16),
            pltpu.VMEM((PART, CTX, BLOCK, SIDE), BF16),
            pltpu.VMEM((3, 8, ROWS), F32),
            pltpu.VMEM((3, SIDE, ROWS), F32),
            pltpu.VMEM((3, ROWS, SIDE), F32),
            pltpu.VMEM((SIDE, ROWS), F32),
            pltpu.VMEM((ROWS, SIDE), F32),
            dma((4,)),
            dma((2, 9)), dma((2, 9)),
            dma((2, 9)), dma((2, 9)),
            dma((9,)), dma((9,)),
            dma((3, 9)), dma((3, 9)),
            dma((8,)), dma((8,)),
            dma((8,)), dma((8,)),
            dma((4,)),
            dma((2,)),
            dma((CTX,)), dma((CTX,)),
            dma((PART, CTX)), dma((PART, CTX)),
            dma((PART, CTX)), dma((PART, CTX)),
        ],
        compiler_params=pltpu.CompilerParams(
            collective_id=0, has_side_effects=True, vmem_limit_bytes=62 * 2**20
        ),
        cost_estimate=pl.CostEstimate(
            flops=2 * (3 * ROWS * TP * ROWS * SLAB + TP * ROWS * ROWS * SLAB) + 2_400_000_000,
            bytes_accessed=8 * 2**20,
            transcendentals=0,
        ),
        name="hyena",
    )(
        tokens,
        in_weight,
        jnp.swapaxes(short_taps, 1, 2),
        long_filter,
        skip_gain.reshape(1, ROWS),
        out_weight,
        *tables(),
    )


def solution(mesh):
    placed = (
        P("tp", "ctx"),
        P(None, "ctx", "tp"),
        P(None, "tp", None),
        P("tp", "ctx"),
        P("tp"),
        P("tp", "ctx"),
    )
    return jax.shard_map(
        per_device, mesh=mesh, in_specs=placed, out_specs=P("tp", "ctx"), check_vma=False
    )
```

```python
import functools
import math

import jax
import jax.numpy as jnp
import numpy as np
from jax import lax
from jax.experimental import pallas as pl
from jax.experimental.pallas import tpu as pltpu
from jax.sharding import PartitionSpec as P

MESH = pl.DeviceIdType.MESH
BF16 = jnp.bfloat16
F32 = jnp.float32

RING = 4
PAIR = 2
CTX = 16
TP = 8
ROWS = 512
SLAB = 1024
WROWS = 256
OWN = 32
SIDE = 128
PART = 2
SUB = OWN // PART
HALF = ROWS // PART
PIECES = ((0, 0, HALF), (1, 0, 64), (1, 64, HALF - 64))
BLOCK = SUB * 8

OWN_S, PAIR_S, LEFT, RIGHT, PLEFT, PRIGHT, FAR, PFAR = range(8)
COPIES = {
    "A": (0, OWN_S, PAIR_S, None, "pair"),
    "Bp": (1, OWN_S, LEFT, None, "plus"),
    "Bm": (2, OWN_S, RIGHT, None, "minus"),
    "Cp": (3, PAIR_S, PLEFT, None, "plus"),
    "Cm": (4, PAIR_S, PRIGHT, None, "minus"),
    "Dp": (5, LEFT, FAR, 0, "plus"),
    "Dm": (6, RIGHT, FAR, 1, "minus"),
    "Ep": (7, PLEFT, PFAR, 0, "plus"),
    "Em": (8, PRIGHT, PFAR, 1, "minus"),
    "AL": (3, LEFT, PLEFT, None, "pair"),
    "AR": (4, RIGHT, PRIGHT, None, "pair"),
    "AF0": (7, FAR, PFAR, 0, "pair"),
    "AF1": (8, FAR, PFAR, 1, "pair"),
}


def tables():
    i = np.arange(SIDE)
    quarter = 2 * np.pi * ((i[:, None] * (4 * i[None, :] + 1)) % (4 * SIDE)) / (4 * SIDE)
    plain = 2 * np.pi * ((i[:, None] * i[None, :]) % SIDE) / SIDE
    twist = 2 * np.pi * (((4 * i[:, None] + 1) * i[None, :]) % (4 * SIDE * SIDE)) / (4 * SIDE * SIDE)
    f1 = np.concatenate([np.cos(quarter.T), -np.sin(quarter.T)], 0)
    c, s = np.cos(plain), np.sin(plain)
    f2 = np.block([[c, -s], [s, c]])
    f3 = np.block([[c, s], [-s, c]])
    f4 = np.concatenate([np.cos(quarter), -np.sin(quarter)], 1) / (SIDE * SIDE)
    tw = np.stack([np.cos(twist), np.sin(twist)])
    return [jnp.asarray(a, BF16) for a in (f1, f2, f3, f4)] + [jnp.asarray(tw, F32)]


def rel_slot(dring, dpair):
    return 3 * dring - 7 * (dring // 3) + dpair * (1 + dring % 2)


class Gather:
    def __init__(self, devs, src, dst, got, send_sem, recv_sem):
        self.devs, self.src, self.dst, self.got = devs, src, dst, got
        self.send_sem, self.recv_sem = send_sem, recv_sem
        self.sent = []

    def send(self, *names):
        for name in names:
            i, shard, there, half, to = COPIES[name]
            copy = pltpu.make_async_remote_copy(
                src_ref=self.src(shard, half),
                dst_ref=self.dst(shard, there, half),
                send_sem=self.send_sem.at[i],
                recv_sem=self.recv_sem.at[i],
                device_id=self.devs[to],
                device_id_type=MESH,
            )
            copy.start()
            self.sent.append(copy)

    def recv(self, *names):
        for name in names:
            i, _, there, half, to = COPIES[name]
            ref = self.got(there, half)
            pltpu.make_async_copy(ref, ref, self.recv_sem.at[i]).wait()

    def finish(self):
        for copy in self.sent:
            copy.wait_send()


def dot(a, b):
    return jnp.dot(a, b, preferred_element_type=F32)


def kernel(
    tok, w, taps, filt, skip, ow, f1, f2, f3, f4, tw,
    out,
    tok_all, w_all, ow_all, hid_all, acc, w_st, ow_st, ow_send, ow_held,
    fsend, frecv, gated, gsend, grecv, xf, spec, lsend, lrecv,
    halo_send, halo_recv, halo_t, rows_t, taps_t,
    local_sem, tok_ss, tok_rs, w_ss, w_rs, ow_ss, ow_rs, h_ss, h_rs, w_sib_ss, w_sib_rs, ow_sib_ss, ow_sib_rs,
    swap_sem, halo_sem, f_ss, f_rs, g_ss, g_rs, l_ss, l_rs,
):
    ctx, tp = lax.axis_index("ctx"), lax.axis_index("tp")
    y_lo, z, core = ctx // 8, (ctx // 2) % 4, ctx % 2
    y_hi, x = tp // 4, tp % 4

    def ctx_at(y, zz, c):
        return y * 8 + zz * 2 + c

    tp_devs = {
        "pair": (ctx, (1 - y_hi) * 4 + x),
        "plus": (ctx, y_hi * 4 + (x + 1) % 4),
        "minus": (ctx, y_hi * 4 + (x + 3) % 4),
    }
    ctx_devs = {
        "pair": (ctx_at(1 - y_lo, z, core), tp),
        "plus": (ctx_at(y_lo, (z + 1) % 4, core), tp),
        "minus": (ctx_at(y_lo, (z + 3) % 4, core), tp),
    }
    sibling = (ctx_at(y_lo, z, 1 - core), tp)
    cross_dev = (ctx_at(y_hi, (z + x) % 4, core), y_lo * 4 + x)
    cross_from = (ctx_at(y_hi, (z + 4 - x) % 4, core), y_lo * 4 + x)
    cross_group = y_hi != y_lo
    cross_away = jnp.logical_or(cross_group, x != 0)
    swap_dev = (ctx, y_hi * 4 + (z + 4 - x) % 4)
    swap_by = (z + 8 - 2 * x) % 4
    swap_away = swap_by != 0
    swap_far = swap_by == 2

    local = [
        pltpu.make_async_copy(w, w_st, local_sem.at[0]),
        pltpu.make_async_copy(ow, ow_st, local_sem.at[1]),
        pltpu.make_async_copy(filt, acc.at[0], local_sem.at[2]),
        pltpu.make_async_copy(tok, tok_all.at[pl.ds(0, ROWS)], local_sem.at[3]),
    ]
    for copy in local:
        copy.start()
    halo_recv[...] = jnp.zeros_like(halo_recv)

    barrier = pltpu.get_barrier_semaphore()
    for i in range(1, CTX):
        pl.semaphore_signal(barrier, inc=1, device_id=((ctx + i) % CTX, tp), device_id_type=MESH)
    for d in tp_devs.values():
        pl.semaphore_signal(barrier, inc=1, device_id=d, device_id_type=MESH)

    @pl.when(cross_group)
    def _():
        pl.semaphore_signal(barrier, inc=1, device_id=cross_from, device_id_type=MESH)

    @pl.when(swap_far)
    def _():
        pl.semaphore_signal(barrier, inc=1, device_id=swap_dev, device_id_type=MESH)

    pl.semaphore_wait(barrier, CTX - 1 + 3 + cross_group.astype(jnp.int32) + swap_far.astype(jnp.int32))

    def tok_gather(k):
        def rows(shard, half):
            if half is None:
                return pl.ds(shard * ROWS + k * HALF, HALF)
            return pl.ds(shard * ROWS + k * HALF + half * (HALF // 2), HALF // 2)

        def src(shard, half):
            return (tok if shard == OWN_S else tok_all).at[rows(shard, half)]

        return Gather(
            tp_devs, src, lambda shard, there, half: tok_all.at[rows(there, half)],
            lambda there, half: tok_all.at[rows(there, half)], tok_ss.at[k], tok_rs.at[k],
        )

    t_g = [tok_gather(k) for k in range(2)]
    t_g[0].send("Bp", "Bm")

    def w_slot(shard, turns=1):
        dz = {OWN_S: 0, PAIR_S: 0, LEFT: 3, RIGHT: 1, PLEFT: 3, PRIGHT: 1, FAR: 2, PFAR: 2}[shard]
        dy = 1 if shard in (PAIR_S, PLEFT, PRIGHT, PFAR) else 0
        return rel_slot((z + dz + 8 - turns * x) % 4, (y_lo + dy + y_hi) % 2)

    def w_lanes(shard, c):
        return pl.ds(pl.multiple_of(w_slot(shard) * ROWS + c * WROWS, WROWS), WROWS)

    def w_view(shard, half, c=core):
        return w_all.at[:, :, w_lanes(shard, c)]

    def w_gather(k):
        def view(shard, half):
            if half is None:
                return w_all.at[:, pl.ds(k * HALF, HALF), w_lanes(shard, core)]
            return w_all.at[:, pl.ds(k * HALF + half * (HALF // 2), HALF // 2), w_lanes(shard, core)]

        return Gather(ctx_devs, view, lambda shard, there, half: view(shard, half), view, w_ss.at[k], w_rs.at[k])

    w_g = [w_gather(k) for k in range(2)]

    def sib_copy(view, shard, ss, rs):
        return pltpu.make_async_remote_copy(
            src_ref=view(shard, None),
            dst_ref=view(shard, None),
            send_sem=ss.at[shard],
            recv_sem=rs.at[shard],
            device_id=sibling,
            device_id_type=MESH,
        )

    sib_sent = []

    def w_sib(shard):
        copy = sib_copy(w_view, shard, w_sib_ss, w_sib_rs)
        copy.start()
        sib_sent.append(copy)

    local[0].wait()
    for s in range(3):
        w_all[s, :, w_lanes(OWN_S, core)] = w_st[s].T
    w_g[0].send("A", "Bp", "Bm")
    w_g[1].send("A")
    w_sib(OWN_S)

    def ow_view(shard, half, c=core):
        lanes = pl.ds(pl.multiple_of(w_slot(shard, 2) * HALF, HALF), HALF)
        rows = pl.ds(pl.multiple_of(c * WROWS, WROWS), WROWS)
        if half is None:
            return ow_all.at[:, rows, lanes]
        return ow_all.at[half, rows, lanes]

    local[1].wait()
    for h in range(PART):
        picked = jnp.concatenate([ow_st[pl.ds(d * OWN + h * SUB, SUB), :] for d in range(CTX)], axis=0)
        ow_send[h] = picked.T
    cross = pltpu.make_async_remote_copy(
        src_ref=ow_send,
        dst_ref=ow_held,
        send_sem=swap_sem.at[0],
        recv_sem=swap_sem.at[1],
        device_id=cross_dev,
        device_id_type=MESH,
    )

    swap_lanes = pl.ds(pl.multiple_of(rel_slot((2 * x + 4 - z) % 4, (y_hi + y_lo) % 2) * HALF, HALF), HALF)
    swap_rows = pl.ds(pl.multiple_of(core * WROWS, WROWS), WROWS)
    swap = pltpu.make_async_remote_copy(
        src_ref=ow_held,
        dst_ref=ow_all.at[:, swap_rows, swap_lanes],
        send_sem=swap_sem.at[2],
        recv_sem=swap_sem.at[3],
        device_id=swap_dev,
        device_id_type=MESH,
    )

    rows_t[...] = jnp.zeros_like(rows_t)
    for s in range(3):
        for j in range(3):
            rows_t[3 * s + j : 3 * s + j + 1, :] = taps[s, j : j + 1, :]
    rows_t[9:10, :] = skip[...]
    taps_t[...] = rows_t[...].T

    local[2].wait()

    @pl.loop(0, ROWS // SUB)
    def _(b):
        v = acc[0, pl.ds(pl.multiple_of(b * SUB, SUB), SUB), :]
        fsend[pl.ds(pl.multiple_of(b * BLOCK, BLOCK), BLOCK), :] = v.reshape(BLOCK, SIDE).astype(BF16)

    def to_each(start):
        @pl.loop(0, CTX)
        def _(d):
            @pl.when(d != ctx)
            def _():
                start(d, True)

            @pl.when(d == ctx)
            def _():
                start(d, False)

    def filter_copy(d, remote):
        src = fsend.at[pl.ds(pl.multiple_of(d * 2 * BLOCK, 2 * BLOCK), 2 * BLOCK)]
        dst = frecv.at[ctx]
        if remote:
            return pltpu.make_async_remote_copy(
                src_ref=src, dst_ref=dst, send_sem=f_ss.at[d], recv_sem=f_rs.at[ctx],
                device_id=(d, tp), device_id_type=MESH,
            )
        return pltpu.make_async_copy(src, dst, f_rs.at[ctx])

    def part_copy(src_ref, dst_ref, ss, rs, h, d, remote):
        src, dst = src_ref.at[h, d], dst_ref.at[h, ctx]
        if remote:
            return pltpu.make_async_remote_copy(
                src_ref=src, dst_ref=dst, send_sem=ss.at[h, d], recv_sem=rs.at[h, ctx],
                device_id=(d, tp), device_id_type=MESH,
            )
        return pltpu.make_async_copy(src, dst, rs.at[h, ctx])

    w_g[0].recv("Bp", "Bm")
    w_g[1].send("Bp", "Bm")
    w_g[0].send("Dp", "Dm")
    t_g[0].send("A")
    t_g[1].send("Bp", "Bm")
    t_g[0].recv("Bp", "Bm")
    t_g[0].send("Dp", "Dm")
    t_g[1].send("A")
    w_g[1].recv("Bp", "Bm")
    w_g[1].send("Dp", "Dm")
    w_sib(LEFT)
    w_sib(RIGHT)
    w_g[0].recv("A")
    w_g[0].send("Cp", "Cm")
    w_g[1].recv("A")
    w_g[1].send("Cp", "Cm")
    w_sib(PAIR_S)
    t_g[0].recv("A")
    t_g[0].send("Cp", "Cm")
    t_g[1].recv("Bp", "Bm")
    t_g[1].send("Dp", "Dm")
    w_g[0].recv("Cp", "Cm")
    w_g[0].send("Ep", "Em")
    t_g[1].recv("A")
    t_g[1].send("Cp", "Cm")

    @pl.when(cross_away)
    def _():
        cross.start()

    @pl.when(jnp.logical_not(cross_away))
    def _():
        pltpu.make_async_copy(ow_send, ow_held, swap_sem.at[1]).start()

    w_g[1].recv("Cp", "Cm")
    w_g[1].send("Ep", "Em")
    w_sib(PLEFT)
    w_sib(PRIGHT)
    for g in w_g:
        g.recv("Dp", "Dm")
    w_sib(FAR)
    t_g[0].recv("Cp", "Cm")
    t_g[0].send("Ep", "Em")
    for g in w_g:
        g.recv("Ep", "Em")
    w_sib(PFAR)
    to_each(lambda d, remote: filter_copy(d, remote).start())
    t_g[1].recv("Cp", "Cm")
    t_g[1].send("Ep", "Em")
    for shard in range(8):
        ref = w_view(shard, None, 1 - core)
        pltpu.make_async_copy(ref, ref, w_sib_rs.at[shard]).wait()
    local[3].wait()

    early, late = 6 * ROWS, 2 * ROWS

    @pl.loop(0, 8)
    def _(i):
        s, lanes = 1 + i // 4, pl.ds(pl.multiple_of((i % 4) * 256, 256), 256)
        acc[s, :, lanes] = dot(w_all[s, :, pl.ds(0, early)], tok_all[pl.ds(0, early), lanes])

    def forward(c):
        pair = jnp.concatenate([xf[c].astype(BF16), xf[c + 1].astype(BF16)], axis=1)
        a = dot(f1[...], pair)
        cos, sin = tw[0], tw[1]
        turned = []
        for j in range(2):
            re, im = a[:SIDE, j * SIDE : (j + 1) * SIDE], a[SIDE:, j * SIDE : (j + 1) * SIDE]
            turned.append(jnp.concatenate([re * cos + im * sin, im * cos - re * sin], axis=1).astype(BF16))
        return dot(jnp.concatenate(turned, axis=0), f2[...])

    for g in t_g:
        g.recv("Dp", "Dm", "Ep", "Em")

    pltpu.make_async_copy(ow_held, ow_held, swap_sem.at[1]).wait()

    @pl.when(swap_away)
    def _():
        swap.start()

    @pl.when(jnp.logical_not(swap_away))
    def _():
        pltpu.make_async_copy(ow_held, ow_view(OWN_S, None), swap_sem.at[3]).start()

    def finish_tile(s, n):
        lanes = pl.ds(pl.multiple_of(n * 256, 256), 256)
        acc[s, :, lanes] = acc[s, :, lanes] + dot(
            w_all[s, :, pl.ds(early, late)], tok_all[pl.ds(early, late), lanes]
        )

    def halo_copy(first, count, i):
        return pltpu.make_async_remote_copy(
            src_ref=halo_send.at[pl.ds(first, count)],
            dst_ref=halo_recv.at[pl.ds(first, count), pl.ds(SIDE - 8, 8)],
            send_sem=halo_sem.at[2 * i],
            recv_sem=halo_sem.at[2 * i + 1],
            device_id=((ctx + 1) % CTX, tp),
            device_id_type=MESH,
        )

    @pl.loop(1, 3)
    def _(s):
        finish_tile(s, 3)
        halo_send[s] = acc[s, :, pl.ds(SLAB - SIDE, SIDE)].T[SIDE - 8 :]

    halo = halo_copy(1, 2, 0)
    halo.start()

    @pl.loop(0, 6)
    def _(i):
        finish_tile(1 + i // 3, i % 3)

    halo.wait_recv()
    for s in (1, 2):
        halo_t[s] = jnp.where(ctx > 0, halo_recv[s].T, 0.0)

    def short(s, r0):
        rows = pl.ds(r0, SUB)
        p = acc[s, rows, :]
        e = jnp.concatenate([halo_t[s, rows, :], p], axis=1)
        one = pltpu.roll(e, 1, 1)[:, SIDE:]
        two = pltpu.roll(e, 2, 1)[:, SIDE:]
        tap = taps_t[rows, :]
        return (
            tap[:, 3 * s : 3 * s + 1] * p
            + tap[:, 3 * s + 1 : 3 * s + 2] * one
            + tap[:, 3 * s + 2 : 3 * s + 3] * two
        )

    for h in range(PART):

        @pl.loop(0, CTX)
        def _(d):
            r0 = pl.multiple_of(d * OWN + h * SUB, SUB)
            g = (short(1, r0) * short(2, r0)).astype(BF16)
            gated[pl.ds(r0, SUB), :] = g
            gsend[h, d] = g.astype(F32).reshape(BLOCK, SIDE).astype(BF16)

            @pl.when(d != ctx)
            def _():
                part_copy(gsend, grecv, g_ss, g_rs, h, d, True).start()

            @pl.when(d == ctx)
            def _():
                part_copy(gsend, grecv, g_ss, g_rs, h, d, False).start()

    ow_g = Gather(ctx_devs, ow_view, lambda shard, there, half: ow_view(shard, half), ow_view, ow_ss, ow_rs)

    def ow_sib(shard):
        copy = sib_copy(ow_view, shard, ow_sib_ss, ow_sib_rs)
        copy.start()
        sib_sent.append(copy)

    @pl.loop(0, 4)
    def _(n):
        lanes = pl.ds(pl.multiple_of((3 - n) * 256, 256), 256)
        acc[0, :, lanes] = dot(w_all[0], tok_all[:, lanes])

    halo_send[0] = acc[0, :, pl.ds(SLAB - SIDE, SIDE)].T[SIDE - 8 :]
    halo_zero = halo_copy(0, 1, 1)
    halo_zero.start()

    @pl.loop(0, CTX)
    def _(s):
        ref = frecv.at[s]
        pltpu.make_async_copy(ref, ref, f_rs.at[s]).wait()
        xf[:, pl.ds(pl.multiple_of(s * 8, 8), 8), :] = frecv[s].astype(F32).reshape(OWN, 8, SIDE)

    @pl.loop(0, OWN // 2, unroll=4)
    def _(i):
        spec[i] = forward(2 * i)

    def take(h):
        part = pl.ds(h * SUB, SUB)

        @pl.loop(0, CTX)
        def _(s):
            ref = grecv.at[h, s]
            pltpu.make_async_copy(ref, ref, g_rs.at[h, s]).wait()
            xf[part, pl.ds(pl.multiple_of(s * 8, 8), 8), :] = grecv[h, s].astype(F32).reshape(SUB, 8, SIDE)

    def convolve(h):
        part = pl.ds(h * SUB, SUB)

        @pl.loop(0, SUB // 2, unroll=4)
        def _(i):
            c = h * SUB + 2 * i
            x_f, h_f = forward(c), spec[h * (SUB // 2) + i]
            xr, xi, hr, hi = x_f[:, :SIDE], x_f[:, SIDE:], h_f[:, :SIDE], h_f[:, SIDE:]
            prod = jnp.concatenate([xr * hr - xi * hi, xr * hi + xi * hr], axis=1).astype(BF16)
            b = dot(prod, f3[...])
            cos, sin = tw[0], tw[1]
            back = []
            for j in range(2):
                re, im = b[j * SIDE : (j + 1) * SIDE, :SIDE], b[j * SIDE : (j + 1) * SIDE, SIDE:]
                back.append(jnp.concatenate([re * cos - im * sin, im * cos + re * sin], axis=0).astype(BF16))
            y = dot(f4[...], jnp.concatenate(back, axis=1))
            xf[c] = y[:, :SIDE]
            xf[c + 1] = y[:, SIDE:]

        @pl.loop(0, CTX)
        def _(d):
            v = xf[part, pl.ds(pl.multiple_of(d * 8, 8), 8), :]
            lsend[h, d] = v.reshape(BLOCK, SIDE).astype(BF16)

            @pl.when(d != ctx)
            def _():
                part_copy(lsend, lrecv, l_ss, l_rs, h, d, True).start()

            @pl.when(d == ctx)
            def _():
                part_copy(lsend, lrecv, l_ss, l_rs, h, d, False).start()

    def hid_gather(i):
        h, first, count = PIECES[i]

        def view(shard, half):
            if half is None:
                return hid_all.at[h, pl.ds(shard * HALF + first, count)]
            return hid_all.at[h, pl.ds(shard * HALF + first + half * (count // 2), count // 2)]

        return Gather(
            tp_devs, view, lambda shard, there, half: view(there, half), view, h_ss.at[i], h_rs.at[i]
        )

    h_g = [hid_gather(i) for i in range(len(PIECES))]

    def last_stream(h):
        @pl.loop(0, CTX)
        def _(d):
            r0 = pl.multiple_of(d * OWN + h * SUB, SUB)
            acc[0, pl.ds(r0, SUB), :] = short(0, r0)

    def hidden(h):
        @pl.loop(0, CTX)
        def _(d):
            ref = lrecv.at[h, d]
            pltpu.make_async_copy(ref, ref, l_rs.at[h, d]).wait()
            rows = pl.ds(pl.multiple_of(d * OWN + h * SUB, SUB), SUB)
            long_rows = lrecv[h, d].astype(F32).reshape(SUB, SLAB)
            gain = taps_t[rows, :][:, 9:10]
            v = (long_rows + gain * gated[rows, :].astype(F32)) * acc[0, rows, :]
            hid_all[h, pl.ds(pl.multiple_of(d * SUB, SUB), SUB), :] = v.astype(BF16)

    take(0)
    convolve(0)
    ref = ow_view(OWN_S, None)
    pltpu.make_async_copy(ref, ref, swap_sem.at[3]).wait()
    take(1)
    ow_g.send("A", "Bp", "Bm")
    ow_sib(OWN_S)
    convolve(1)
    halo_zero.wait_recv()
    halo_t[0] = jnp.where(ctx > 0, halo_recv[0].T, 0.0)
    last_stream(0)
    hidden(0)
    h_g[0].send("A", "Bp", "Bm")
    ow_g.recv("Bp", "Bm")
    ow_g.send("Dp", "Dm")
    ow_sib(LEFT)
    ow_sib(RIGHT)
    ow_g.recv("A")
    ow_g.send("Cp", "Cm")
    ow_sib(PAIR_S)
    last_stream(1)
    hidden(1)
    h_g[2].send("Bp", "Bm", "A")
    h_g[1].send("A", "Bp", "Bm")
    ow_g.recv("Cp", "Cm")
    ow_g.send("Ep", "Em")
    ow_sib(PLEFT)
    ow_sib(PRIGHT)
    h_g[0].recv("Bp", "Bm")
    h_g[0].send("Dp", "Dm")
    h_g[0].recv("A")
    h_g[0].send("Cp", "Cm")
    ow_g.recv("Dp", "Dm")
    ow_sib(FAR)
    ow_g.recv("Ep", "Em")
    ow_sib(PFAR)
    h_g[2].recv("Bp")
    h_g[2].send("Dp", "AL")
    h_g[2].recv("Bm")
    h_g[2].send("Dm", "AR")
    h_g[1].recv("Bp", "Bm")
    h_g[1].send("Dp", "Dm")
    h_g[1].recv("A")
    h_g[1].send("Cp", "Cm")
    h_g[0].recv("Cp", "Cm")
    h_g[0].send("Ep", "Em")
    h_g[2].recv("Dp")
    h_g[2].send("AF0")
    h_g[2].recv("Dm")
    h_g[2].send("AF1")
    h_g[1].recv("Cp", "Cm")
    h_g[1].send("Ep", "Em")
    for shard in range(8):
        ref = ow_view(shard, None, 1 - core)
        pltpu.make_async_copy(ref, ref, ow_sib_rs.at[shard]).wait()

    def outward(h, k0, k1, first, last):
        @pl.loop(0, 4)
        def _(n):
            lanes = pl.ds(pl.multiple_of(n * 256, 256), 256)
            v = dot(ow_all[h, :, pl.ds(k0, k1 - k0)], hid_all[h, pl.ds(k0, k1 - k0), lanes])
            if not first:
                v = v + acc[1, :, lanes]
            if last:
                out[:, lanes] = v.astype(BF16)
            else:
                acc[1, :, lanes] = v

    outward(0, 0, 6 * HALF, True, False)
    h_g[0].recv("Dp", "Dm", "Ep", "Em")
    outward(0, 6 * HALF, 8 * HALF, False, False)
    h_g[2].recv("A", "AL", "AR")
    outward(1, 0, 6 * HALF, False, False)
    h_g[1].recv("Dp", "Dm", "Ep", "Em")
    h_g[2].recv("AF0", "AF1")
    outward(1, 6 * HALF, 8 * HALF, False, True)

    for gather in (*t_g, *w_g, ow_g, *h_g):
        gather.finish()
    for copy in sib_sent:
        copy.wait_send()

    @pl.when(cross_away)
    def _():
        cross.wait_send()

    @pl.when(swap_away)
    def _():
        swap.wait_send()

    halo.wait_send()
    halo_zero.wait_send()

    @pl.loop(0, CTX)
    def _(d):
        @pl.when(d != ctx)
        def _():
            filter_copy(d, True).wait_send()
            for h in range(PART):
                part_copy(gsend, grecv, g_ss, g_rs, h, d, True).wait_send()
                part_copy(lsend, lrecv, l_ss, l_rs, h, d, True).wait_send()


def per_device(tokens, in_weight, short_taps, long_filter, skip_gain, out_weight):
    hbm = pl.BlockSpec(memory_space=pl.ANY)
    vmem = pl.BlockSpec(memory_space=pltpu.VMEM)
    dma = pltpu.SemaphoreType.DMA
    return pl.pallas_call(
        kernel,
        out_shape=jax.ShapeDtypeStruct((ROWS, SLAB), BF16),
        in_specs=[hbm, hbm, vmem, hbm, vmem, hbm, vmem, vmem, vmem, vmem, vmem],
        out_specs=vmem,
        scratch_shapes=[
            pltpu.VMEM((TP * ROWS, SLAB), BF16),
            pltpu.VMEM((3, ROWS, TP * ROWS), BF16),
            pltpu.VMEM((PART, ROWS, TP * HALF), BF16),
            pltpu.VMEM((PART, TP * HALF, SLAB), BF16),
            pltpu.VMEM((3, ROWS, SLAB), F32),
            pltpu.VMEM((3, WROWS, ROWS), BF16),
            pltpu.VMEM((ROWS, WROWS), BF16),
            pltpu.VMEM((PART, WROWS, HALF), BF16),
            pltpu.VMEM((PART, WROWS, HALF), BF16),
            pltpu.VMEM((ROWS * 8, SIDE), BF16),
            pltpu.VMEM((CTX, 2 * BLOCK, SIDE), BF16),
            pltpu.VMEM((ROWS, SLAB), BF16),
            pltpu.VMEM((PART, CTX, BLOCK, SIDE), BF16),
            pltpu.VMEM((PART, CTX, BLOCK, SIDE), BF16),
            pltpu.VMEM((OWN, SIDE, SIDE), F32),
            pltpu.VMEM((OWN // 2, 2 * SIDE, 2 * SIDE), F32),
            pltpu.VMEM((PART, CTX, BLOCK, SIDE), BF16),
            pltpu.VMEM((PART, CTX, BLOCK, SIDE), BF16),
            pltpu.VMEM((3, 8, ROWS), F32),
            pltpu.VMEM((3, SIDE, ROWS), F32),
            pltpu.VMEM((3, ROWS, SIDE), F32),
            pltpu.VMEM((SIDE, ROWS), F32),
            pltpu.VMEM((ROWS, SIDE), F32),
            dma((4,)),
            dma((2, 9)), dma((2, 9)),
            dma((2, 9)), dma((2, 9)),
            dma((9,)), dma((9,)),
            dma((3, 9)), dma((3, 9)),
            dma((8,)), dma((8,)),
            dma((8,)), dma((8,)),
            dma((4,)),
            dma((4,)),
            dma((CTX,)), dma((CTX,)),
            dma((PART, CTX)), dma((PART, CTX)),
            dma((PART, CTX)), dma((PART, CTX)),
        ],
        compiler_params=pltpu.CompilerParams(
            collective_id=0, has_side_effects=True, vmem_limit_bytes=62 * 2**20
        ),
        cost_estimate=pl.CostEstimate(
            flops=2 * (3 * ROWS * TP * ROWS * SLAB + TP * ROWS * ROWS * SLAB) + 2_400_000_000,
            bytes_accessed=8 * 2**20,
            transcendentals=0,
        ),
        name="hyena",
    )(
        tokens,
        in_weight,
        jnp.swapaxes(short_taps, 1, 2),
        long_filter,
        skip_gain.reshape(1, ROWS),
        out_weight,
        *tables(),
    )


def solution(mesh):
    placed = (
        P("tp", "ctx"),
        P(None, "ctx", "tp"),
        P(None, "tp", None),
        P("tp", "ctx"),
        P("tp"),
        P("tp", "ctx"),
    )
    return jax.shard_map(
        per_device, mesh=mesh, in_specs=placed, out_specs=P("tp", "ctx"), check_vma=False
    )
```

```python
import functools
import math

import jax
import jax.numpy as jnp
import numpy as np
from jax import lax
from jax.experimental import pallas as pl
from jax.experimental.pallas import tpu as pltpu
from jax.sharding import PartitionSpec as P

MESH = pl.DeviceIdType.MESH
BF16 = jnp.bfloat16
F32 = jnp.float32

RING = 4
PAIR = 2
CTX = 16
TP = 8
ROWS = 512
SLAB = 1024
WROWS = 256
OWN = 32
SIDE = 128
PART = 2
SUB = OWN // PART
HALF = ROWS // PART
PIECES = ((0, 0, HALF), (1, 0, 64), (1, 64, HALF - 64))
BLOCK = SUB * 8

OWN_S, PAIR_S, LEFT, RIGHT, PLEFT, PRIGHT, FAR, PFAR = range(8)
COPIES = {
    "A": (0, OWN_S, PAIR_S, None, "pair"),
    "Bp": (1, OWN_S, LEFT, None, "plus"),
    "Bm": (2, OWN_S, RIGHT, None, "minus"),
    "Cp": (3, PAIR_S, PLEFT, None, "plus"),
    "Cm": (4, PAIR_S, PRIGHT, None, "minus"),
    "Dp": (5, LEFT, FAR, 0, "plus"),
    "Dm": (6, RIGHT, FAR, 1, "minus"),
    "Ep": (7, PLEFT, PFAR, 0, "plus"),
    "Em": (8, PRIGHT, PFAR, 1, "minus"),
    "AL": (3, LEFT, PLEFT, None, "pair"),
    "AR": (4, RIGHT, PRIGHT, None, "pair"),
    "AF0": (7, FAR, PFAR, 0, "pair"),
    "AF1": (8, FAR, PFAR, 1, "pair"),
}


def tables():
    i = np.arange(SIDE)
    quarter = 2 * np.pi * ((i[:, None] * (4 * i[None, :] + 1)) % (4 * SIDE)) / (4 * SIDE)
    plain = 2 * np.pi * ((i[:, None] * i[None, :]) % SIDE) / SIDE
    twist = 2 * np.pi * (((4 * i[:, None] + 1) * i[None, :]) % (4 * SIDE * SIDE)) / (4 * SIDE * SIDE)
    f1 = np.concatenate([np.cos(quarter.T), -np.sin(quarter.T)], 0)
    c, s = np.cos(plain), np.sin(plain)
    f2 = np.block([[c, -s], [s, c]])
    f3 = np.block([[c, s], [-s, c]])
    f4 = np.concatenate([np.cos(quarter), -np.sin(quarter)], 1) / (SIDE * SIDE)
    tw = np.stack([np.cos(twist), np.sin(twist)])
    return [jnp.asarray(a, BF16) for a in (f1, f2, f3, f4)] + [jnp.asarray(tw, F32)]


def rel_slot(dring, dpair):
    return 3 * dring - 7 * (dring // 3) + dpair * (1 + dring % 2)


class Gather:
    def __init__(self, devs, src, dst, got, send_sem, recv_sem):
        self.devs, self.src, self.dst, self.got = devs, src, dst, got
        self.send_sem, self.recv_sem = send_sem, recv_sem
        self.sent = []

    def send(self, *names):
        for name in names:
            i, shard, there, half, to = COPIES[name]
            copy = pltpu.make_async_remote_copy(
                src_ref=self.src(shard, half),
                dst_ref=self.dst(shard, there, half),
                send_sem=self.send_sem.at[i],
                recv_sem=self.recv_sem.at[i],
                device_id=self.devs[to],
                device_id_type=MESH,
            )
            copy.start()
            self.sent.append(copy)

    def recv(self, *names):
        for name in names:
            i, _, there, half, to = COPIES[name]
            ref = self.got(there, half)
            pltpu.make_async_copy(ref, ref, self.recv_sem.at[i]).wait()

    def finish(self):
        for copy in self.sent:
            copy.wait_send()


def dot(a, b):
    return jnp.dot(a, b, preferred_element_type=F32)


def kernel(
    tok, w, taps, filt, skip, ow, f1, f2, f3, f4, tw,
    out,
    tok_all, w_all, ow_all, hid_all, acc, w_st, ow_st, ow_send, ow_held,
    fsend, frecv, gated, gsend, grecv, xf, spec, lsend, lrecv,
    halo_send, halo_recv, halo_t, rows_t, taps_t,
    local_sem, tok_ss, tok_rs, w_ss, w_rs, ow_ss, ow_rs, h_ss, h_rs, w_sib_ss, w_sib_rs, ow_sib_ss, ow_sib_rs,
    swap_sem, halo_sem, f_ss, f_rs, g_ss, g_rs, l_ss, l_rs,
):
    ctx, tp = lax.axis_index("ctx"), lax.axis_index("tp")
    y_lo, z, core = ctx // 8, (ctx // 2) % 4, ctx % 2
    y_hi, x = tp // 4, tp % 4

    def ctx_at(y, zz, c):
        return y * 8 + zz * 2 + c

    tp_devs = {
        "pair": (ctx, (1 - y_hi) * 4 + x),
        "plus": (ctx, y_hi * 4 + (x + 1) % 4),
        "minus": (ctx, y_hi * 4 + (x + 3) % 4),
    }
    ctx_devs = {
        "pair": (ctx_at(1 - y_lo, z, core), tp),
        "plus": (ctx_at(y_lo, (z + 1) % 4, core), tp),
        "minus": (ctx_at(y_lo, (z + 3) % 4, core), tp),
    }
    sibling = (ctx_at(y_lo, z, 1 - core), tp)
    cross_dev = (ctx_at(y_hi, (z + x) % 4, core), y_lo * 4 + x)
    cross_from = (ctx_at(y_hi, (z + 4 - x) % 4, core), y_lo * 4 + x)
    cross_group = y_hi != y_lo
    cross_away = jnp.logical_or(cross_group, x != 0)
    swap_dev = (ctx, y_hi * 4 + (z + 4 - x) % 4)
    swap_by = (z + 8 - 2 * x) % 4
    swap_away = swap_by != 0
    swap_far = swap_by == 2

    local = [
        pltpu.make_async_copy(w, w_st, local_sem.at[0]),
        pltpu.make_async_copy(ow, ow_st, local_sem.at[1]),
        pltpu.make_async_copy(filt, acc.at[0], local_sem.at[2]),
        pltpu.make_async_copy(tok, tok_all.at[pl.ds(0, ROWS)], local_sem.at[3]),
    ]
    for copy in local:
        copy.start()
    halo_recv[...] = jnp.zeros_like(halo_recv)

    barrier = pltpu.get_barrier_semaphore()
    for i in range(1, CTX):
        pl.semaphore_signal(barrier, inc=1, device_id=((ctx + i) % CTX, tp), device_id_type=MESH)
    for d in tp_devs.values():
        pl.semaphore_signal(barrier, inc=1, device_id=d, device_id_type=MESH)

    @pl.when(cross_group)
    def _():
        pl.semaphore_signal(barrier, inc=1, device_id=cross_from, device_id_type=MESH)

    @pl.when(swap_far)
    def _():
        pl.semaphore_signal(barrier, inc=1, device_id=swap_dev, device_id_type=MESH)

    pl.semaphore_wait(barrier, CTX - 1 + 3 + cross_group.astype(jnp.int32) + swap_far.astype(jnp.int32))

    def tok_gather(k):
        def rows(shard, half):
            if half is None:
                return pl.ds(shard * ROWS + k * HALF, HALF)
            return pl.ds(shard * ROWS + k * HALF + half * (HALF // 2), HALF // 2)

        def src(shard, half):
            return (tok if shard == OWN_S else tok_all).at[rows(shard, half)]

        return Gather(
            tp_devs, src, lambda shard, there, half: tok_all.at[rows(there, half)],
            lambda there, half: tok_all.at[rows(there, half)], tok_ss.at[k], tok_rs.at[k],
        )

    t_g = [tok_gather(k) for k in range(2)]
    t_g[0].send("Bp", "Bm")

    def w_slot(shard, turns=1):
        dz = {OWN_S: 0, PAIR_S: 0, LEFT: 3, RIGHT: 1, PLEFT: 3, PRIGHT: 1, FAR: 2, PFAR: 2}[shard]
        dy = 1 if shard in (PAIR_S, PLEFT, PRIGHT, PFAR) else 0
        return rel_slot((z + dz + 8 - turns * x) % 4, (y_lo + dy + y_hi) % 2)

    def w_lanes(shard, c):
        return pl.ds(pl.multiple_of(w_slot(shard) * ROWS + c * WROWS, WROWS), WROWS)

    def w_view(shard, half, c=core):
        return w_all.at[:, :, w_lanes(shard, c)]

    def w_gather(k):
        def view(shard, half):
            if half is None:
                return w_all.at[:, pl.ds(k * HALF, HALF), w_lanes(shard, core)]
            return w_all.at[:, pl.ds(k * HALF + half * (HALF // 2), HALF // 2), w_lanes(shard, core)]

        return Gather(ctx_devs, view, lambda shard, there, half: view(shard, half), view, w_ss.at[k], w_rs.at[k])

    w_g = [w_gather(k) for k in range(2)]

    def sib_copy(view, shard, ss, rs):
        return pltpu.make_async_remote_copy(
            src_ref=view(shard, None),
            dst_ref=view(shard, None),
            send_sem=ss.at[shard],
            recv_sem=rs.at[shard],
            device_id=sibling,
            device_id_type=MESH,
        )

    sib_sent = []

    def w_sib(shard):
        copy = sib_copy(w_view, shard, w_sib_ss, w_sib_rs)
        copy.start()
        sib_sent.append(copy)

    local[0].wait()
    for s in range(3):
        w_all[s, :, w_lanes(OWN_S, core)] = w_st[s].T
    w_g[0].send("A", "Bp", "Bm")
    w_g[1].send("A")
    w_sib(OWN_S)

    def ow_view(shard, half, c=core):
        lanes = pl.ds(pl.multiple_of(w_slot(shard, 2) * HALF, HALF), HALF)
        rows = pl.ds(pl.multiple_of(c * WROWS, WROWS), WROWS)
        if half is None:
            return ow_all.at[:, rows, lanes]
        return ow_all.at[half, rows, lanes]

    local[1].wait()
    for h in range(PART):
        picked = jnp.concatenate([ow_st[pl.ds(d * OWN + h * SUB, SUB), :] for d in range(CTX)], axis=0)
        ow_send[h] = picked.T
    cross = pltpu.make_async_remote_copy(
        src_ref=ow_send,
        dst_ref=ow_held,
        send_sem=swap_sem.at[0],
        recv_sem=swap_sem.at[1],
        device_id=cross_dev,
        device_id_type=MESH,
    )

    swap_lanes = pl.ds(pl.multiple_of(rel_slot((2 * x + 4 - z) % 4, (y_hi + y_lo) % 2) * HALF, HALF), HALF)
    swap_rows = pl.ds(pl.multiple_of(core * WROWS, WROWS), WROWS)
    swap = pltpu.make_async_remote_copy(
        src_ref=ow_held,
        dst_ref=ow_all.at[:, swap_rows, swap_lanes],
        send_sem=swap_sem.at[2],
        recv_sem=swap_sem.at[3],
        device_id=swap_dev,
        device_id_type=MESH,
    )

    rows_t[...] = jnp.zeros_like(rows_t)
    for s in range(3):
        for j in range(3):
            rows_t[3 * s + j : 3 * s + j + 1, :] = taps[s, j : j + 1, :]
    rows_t[9:10, :] = skip[...]
    taps_t[...] = rows_t[...].T

    local[2].wait()

    @pl.loop(0, ROWS // SUB)
    def _(b):
        v = acc[0, pl.ds(pl.multiple_of(b * SUB, SUB), SUB), :]
        fsend[pl.ds(pl.multiple_of(b * BLOCK, BLOCK), BLOCK), :] = v.reshape(BLOCK, SIDE).astype(BF16)

    def to_each(start):
        @pl.loop(0, CTX)
        def _(d):
            @pl.when(d != ctx)
            def _():
                start(d, True)

            @pl.when(d == ctx)
            def _():
                start(d, False)

    def filter_copy(d, remote):
        src = fsend.at[pl.ds(pl.multiple_of(d * 2 * BLOCK, 2 * BLOCK), 2 * BLOCK)]
        dst = frecv.at[ctx]
        if remote:
            return pltpu.make_async_remote_copy(
                src_ref=src, dst_ref=dst, send_sem=f_ss.at[d], recv_sem=f_rs.at[ctx],
                device_id=(d, tp), device_id_type=MESH,
            )
        return pltpu.make_async_copy(src, dst, f_rs.at[ctx])

    def part_copy(src_ref, dst_ref, ss, rs, h, d, remote):
        src, dst = src_ref.at[h, d], dst_ref.at[h, ctx]
        if remote:
            return pltpu.make_async_remote_copy(
                src_ref=src, dst_ref=dst, send_sem=ss.at[h, d], recv_sem=rs.at[h, ctx],
                device_id=(d, tp), device_id_type=MESH,
            )
        return pltpu.make_async_copy(src, dst, rs.at[h, ctx])

    w_g[0].recv("Bp", "Bm")
    w_g[1].send("Bp", "Bm")
    w_g[0].send("Dp", "Dm")
    t_g[0].send("A")
    t_g[1].send("Bp", "Bm")
    t_g[0].recv("Bp", "Bm")
    t_g[0].send("Dp", "Dm")
    t_g[1].send("A")
    w_g[1].recv("Bp", "Bm")
    w_g[1].send("Dp", "Dm")
    w_sib(LEFT)
    w_sib(RIGHT)
    w_g[0].recv("A")
    w_g[0].send("Cp", "Cm")
    w_g[1].recv("A")
    w_g[1].send("Cp", "Cm")
    w_sib(PAIR_S)
    t_g[0].recv("A")
    t_g[0].send("Cp", "Cm")
    t_g[1].recv("Bp", "Bm")
    t_g[1].send("Dp", "Dm")
    w_g[0].recv("Cp", "Cm")
    w_g[0].send("Ep", "Em")
    t_g[1].recv("A")
    t_g[1].send("Cp", "Cm")

    @pl.when(cross_away)
    def _():
        cross.start()

    @pl.when(jnp.logical_not(cross_away))
    def _():
        pltpu.make_async_copy(ow_send, ow_held, swap_sem.at[1]).start()

    w_g[1].recv("Cp", "Cm")
    w_g[1].send("Ep", "Em")
    w_sib(PLEFT)
    w_sib(PRIGHT)
    for g in w_g:
        g.recv("Dp", "Dm")
    w_sib(FAR)
    t_g[0].recv("Cp", "Cm")
    t_g[0].send("Ep", "Em")
    for g in w_g:
        g.recv("Ep", "Em")
    w_sib(PFAR)
    to_each(lambda d, remote: filter_copy(d, remote).start())
    t_g[1].recv("Cp", "Cm")
    t_g[1].send("Ep", "Em")
    for shard in range(8):
        ref = w_view(shard, None, 1 - core)
        pltpu.make_async_copy(ref, ref, w_sib_rs.at[shard]).wait()
    local[3].wait()

    early, late = 6 * ROWS, 2 * ROWS

    @pl.loop(0, 8)
    def _(i):
        s, lanes = 1 + i // 4, pl.ds(pl.multiple_of((i % 4) * 256, 256), 256)
        acc[s, :, lanes] = dot(w_all[s, :, pl.ds(0, early)], tok_all[pl.ds(0, early), lanes])

    def forward(c):
        pair = jnp.concatenate([xf[c].astype(BF16), xf[c + 1].astype(BF16)], axis=1)
        a = dot(f1[...], pair)
        cos, sin = tw[0], tw[1]
        turned = []
        for j in range(2):
            re, im = a[:SIDE, j * SIDE : (j + 1) * SIDE], a[SIDE:, j * SIDE : (j + 1) * SIDE]
            turned.append(jnp.concatenate([re * cos + im * sin, im * cos - re * sin], axis=1).astype(BF16))
        return dot(jnp.concatenate(turned, axis=0), f2[...])

    for g in t_g:
        g.recv("Dp", "Dm", "Ep", "Em")

    def finish_tile(s, n):
        lanes = pl.ds(pl.multiple_of(n * 256, 256), 256)
        acc[s, :, lanes] = acc[s, :, lanes] + dot(
            w_all[s, :, pl.ds(early, late)], tok_all[pl.ds(early, late), lanes]
        )

    def halo_copy(first, count, i):
        return pltpu.make_async_remote_copy(
            src_ref=halo_send.at[pl.ds(first, count)],
            dst_ref=halo_recv.at[pl.ds(first, count), pl.ds(SIDE - 8, 8)],
            send_sem=halo_sem.at[2 * i],
            recv_sem=halo_sem.at[2 * i + 1],
            device_id=((ctx + 1) % CTX, tp),
            device_id_type=MESH,
        )

    @pl.loop(1, 3)
    def _(s):
        finish_tile(s, 3)
        halo_send[s] = acc[s, :, pl.ds(SLAB - SIDE, SIDE)].T[SIDE - 8 :]

    halo = halo_copy(1, 2, 0)
    halo.start()

    @pl.loop(0, 6)
    def _(i):
        finish_tile(1 + i // 3, i % 3)

    halo.wait_recv()
    for s in (1, 2):
        halo_t[s] = jnp.where(ctx > 0, halo_recv[s].T, 0.0)

    def short(s, r0):
        rows = pl.ds(r0, SUB)
        p = acc[s, rows, :]
        e = jnp.concatenate([halo_t[s, rows, :], p], axis=1)
        one = pltpu.roll(e, 1, 1)[:, SIDE:]
        two = pltpu.roll(e, 2, 1)[:, SIDE:]
        tap = taps_t[rows, :]
        return (
            tap[:, 3 * s : 3 * s + 1] * p
            + tap[:, 3 * s + 1 : 3 * s + 2] * one
            + tap[:, 3 * s + 2 : 3 * s + 3] * two
        )

    for h in range(PART):

        @pl.loop(0, CTX, unroll=2)
        def _(d):
            r0 = pl.multiple_of(d * OWN + h * SUB, SUB)
            g = (short(1, r0) * short(2, r0)).astype(BF16)
            gated[pl.ds(r0, SUB), :] = g
            gsend[h, d] = g.astype(F32).reshape(BLOCK, SIDE).astype(BF16)

            @pl.when(d != ctx)
            def _():
                part_copy(gsend, grecv, g_ss, g_rs, h, d, True).start()

            @pl.when(d == ctx)
            def _():
                part_copy(gsend, grecv, g_ss, g_rs, h, d, False).start()

    ow_g = Gather(ctx_devs, ow_view, lambda shard, there, half: ow_view(shard, half), ow_view, ow_ss, ow_rs)

    def ow_sib(shard):
        copy = sib_copy(ow_view, shard, ow_sib_ss, ow_sib_rs)
        copy.start()
        sib_sent.append(copy)

    pltpu.make_async_copy(ow_held, ow_held, swap_sem.at[1]).wait()

    @pl.when(swap_away)
    def _():
        swap.start()

    @pl.when(jnp.logical_not(swap_away))
    def _():
        pltpu.make_async_copy(ow_held, ow_view(OWN_S, None), swap_sem.at[3]).start()

    @pl.loop(0, 4)
    def _(n):
        lanes = pl.ds(pl.multiple_of((3 - n) * 256, 256), 256)
        acc[0, :, lanes] = dot(w_all[0], tok_all[:, lanes])

    halo_send[0] = acc[0, :, pl.ds(SLAB - SIDE, SIDE)].T[SIDE - 8 :]
    halo_zero = halo_copy(0, 1, 1)
    halo_zero.start()

    @pl.loop(0, CTX)
    def _(s):
        ref = frecv.at[s]
        pltpu.make_async_copy(ref, ref, f_rs.at[s]).wait()
        xf[:, pl.ds(pl.multiple_of(s * 8, 8), 8), :] = frecv[s].astype(F32).reshape(OWN, 8, SIDE)

    @pl.loop(0, OWN // 2, unroll=4)
    def _(i):
        spec[i] = forward(2 * i)

    def take(h):
        part = pl.ds(h * SUB, SUB)

        @pl.loop(0, CTX)
        def _(s):
            ref = grecv.at[h, s]
            pltpu.make_async_copy(ref, ref, g_rs.at[h, s]).wait()
            xf[part, pl.ds(pl.multiple_of(s * 8, 8), 8), :] = grecv[h, s].astype(F32).reshape(SUB, 8, SIDE)

    def convolve(h):
        part = pl.ds(h * SUB, SUB)

        @pl.loop(0, SUB // 2, unroll=8)
        def _(i):
            c = h * SUB + 2 * i
            x_f, h_f = forward(c), spec[h * (SUB // 2) + i]
            xr, xi, hr, hi = x_f[:, :SIDE], x_f[:, SIDE:], h_f[:, :SIDE], h_f[:, SIDE:]
            prod = jnp.concatenate([xr * hr - xi * hi, xr * hi + xi * hr], axis=1).astype(BF16)
            b = dot(prod, f3[...])
            cos, sin = tw[0], tw[1]
            back = []
            for j in range(2):
                re, im = b[j * SIDE : (j + 1) * SIDE, :SIDE], b[j * SIDE : (j + 1) * SIDE, SIDE:]
                back.append(jnp.concatenate([re * cos - im * sin, im * cos + re * sin], axis=0).astype(BF16))
            y = dot(f4[...], jnp.concatenate(back, axis=1))
            xf[c] = y[:, :SIDE]
            xf[c + 1] = y[:, SIDE:]

        @pl.loop(0, CTX)
        def _(d):
            v = xf[part, pl.ds(pl.multiple_of(d * 8, 8), 8), :]
            lsend[h, d] = v.reshape(BLOCK, SIDE).astype(BF16)

            @pl.when(d != ctx)
            def _():
                part_copy(lsend, lrecv, l_ss, l_rs, h, d, True).start()

            @pl.when(d == ctx)
            def _():
                part_copy(lsend, lrecv, l_ss, l_rs, h, d, False).start()

    def hid_gather(i):
        h, first, count = PIECES[i]

        def view(shard, half):
            if half is None:
                return hid_all.at[h, pl.ds(shard * HALF + first, count)]
            return hid_all.at[h, pl.ds(shard * HALF + first + half * (count // 2), count // 2)]

        return Gather(
            tp_devs, view, lambda shard, there, half: view(there, half), view, h_ss.at[i], h_rs.at[i]
        )

    h_g = [hid_gather(i) for i in range(len(PIECES))]

    def last_stream(h):
        @pl.loop(0, CTX, unroll=2)
        def _(d):
            r0 = pl.multiple_of(d * OWN + h * SUB, SUB)
            acc[0, pl.ds(r0, SUB), :] = short(0, r0)

    def hidden(h):
        @pl.loop(0, CTX)
        def _(d):
            ref = lrecv.at[h, d]
            pltpu.make_async_copy(ref, ref, l_rs.at[h, d]).wait()
            rows = pl.ds(pl.multiple_of(d * OWN + h * SUB, SUB), SUB)
            long_rows = lrecv[h, d].astype(F32).reshape(SUB, SLAB)
            gain = taps_t[rows, :][:, 9:10]
            v = (long_rows + gain * gated[rows, :].astype(F32)) * acc[0, rows, :]
            hid_all[h, pl.ds(pl.multiple_of(d * SUB, SUB), SUB), :] = v.astype(BF16)

    take(0)
    convolve(0)
    ref = ow_view(OWN_S, None)
    pltpu.make_async_copy(ref, ref, swap_sem.at[3]).wait()
    take(1)
    ow_g.send("A", "Bp", "Bm")
    ow_sib(OWN_S)
    convolve(1)
    halo_zero.wait_recv()
    halo_t[0] = jnp.where(ctx > 0, halo_recv[0].T, 0.0)
    last_stream(0)
    hidden(0)
    h_g[0].send("A", "Bp", "Bm")
    ow_g.recv("Bp", "Bm")
    ow_g.send("Dp", "Dm")
    ow_sib(LEFT)
    ow_sib(RIGHT)
    ow_g.recv("A")
    ow_g.send("Cp", "Cm")
    ow_sib(PAIR_S)
    last_stream(1)
    hidden(1)
    h_g[2].send("Bp", "Bm", "A")
    h_g[1].send("A", "Bp", "Bm")
    ow_g.recv("Cp", "Cm")
    ow_g.send("Ep", "Em")
    ow_sib(PLEFT)
    ow_sib(PRIGHT)
    h_g[0].recv("Bp", "Bm")
    h_g[0].send("Dp", "Dm")
    h_g[0].recv("A")
    h_g[0].send("Cp", "Cm")
    ow_g.recv("Dp", "Dm")
    ow_sib(FAR)
    ow_g.recv("Ep", "Em")
    ow_sib(PFAR)
    h_g[2].recv("Bp")
    h_g[2].send("Dp", "AL")
    h_g[2].recv("Bm")
    h_g[2].send("Dm", "AR")
    h_g[1].recv("Bp", "Bm")
    h_g[1].send("Dp", "Dm")
    h_g[1].recv("A")
    h_g[1].send("Cp", "Cm")
    h_g[0].recv("Cp", "Cm")
    h_g[0].send("Ep", "Em")
    h_g[2].recv("Dp")
    h_g[2].send("AF0")
    h_g[2].recv("Dm")
    h_g[2].send("AF1")
    h_g[1].recv("Cp", "Cm")
    h_g[1].send("Ep", "Em")
    for shard in range(8):
        ref = ow_view(shard, None, 1 - core)
        pltpu.make_async_copy(ref, ref, ow_sib_rs.at[shard]).wait()

    def outward(h, k0, k1, first, last):
        @pl.loop(0, 4)
        def _(n):
            lanes = pl.ds(pl.multiple_of(n * 256, 256), 256)
            v = dot(ow_all[h, :, pl.ds(k0, k1 - k0)], hid_all[h, pl.ds(k0, k1 - k0), lanes])
            if not first:
                v = v + acc[1, :, lanes]
            if last:
                out[:, lanes] = v.astype(BF16)
            else:
                acc[1, :, lanes] = v

    outward(0, 0, 6 * HALF, True, False)
    h_g[0].recv("Dp", "Dm", "Ep", "Em")
    outward(0, 6 * HALF, 8 * HALF, False, False)
    h_g[2].recv("A", "AL", "AR")
    outward(1, 0, 6 * HALF, False, False)
    h_g[1].recv("Dp", "Dm", "Ep", "Em")
    h_g[2].recv("AF0", "AF1")
    outward(1, 6 * HALF, 8 * HALF, False, True)

    for gather in (*t_g, *w_g, ow_g, *h_g):
        gather.finish()
    for copy in sib_sent:
        copy.wait_send()

    @pl.when(cross_away)
    def _():
        cross.wait_send()

    @pl.when(swap_away)
    def _():
        swap.wait_send()

    halo.wait_send()
    halo_zero.wait_send()

    @pl.loop(0, CTX)
    def _(d):
        @pl.when(d != ctx)
        def _():
            filter_copy(d, True).wait_send()
            for h in range(PART):
                part_copy(gsend, grecv, g_ss, g_rs, h, d, True).wait_send()
                part_copy(lsend, lrecv, l_ss, l_rs, h, d, True).wait_send()


def per_device(tokens, in_weight, short_taps, long_filter, skip_gain, out_weight):
    hbm = pl.BlockSpec(memory_space=pl.ANY)
    vmem = pl.BlockSpec(memory_space=pltpu.VMEM)
    dma = pltpu.SemaphoreType.DMA
    return pl.pallas_call(
        kernel,
        out_shape=jax.ShapeDtypeStruct((ROWS, SLAB), BF16),
        in_specs=[hbm, hbm, vmem, hbm, vmem, hbm, vmem, vmem, vmem, vmem, vmem],
        out_specs=vmem,
        scratch_shapes=[
            pltpu.VMEM((TP * ROWS, SLAB), BF16),
            pltpu.VMEM((3, ROWS, TP * ROWS), BF16),
            pltpu.VMEM((PART, ROWS, TP * HALF), BF16),
            pltpu.VMEM((PART, TP * HALF, SLAB), BF16),
            pltpu.VMEM((3, ROWS, SLAB), F32),
            pltpu.VMEM((3, WROWS, ROWS), BF16),
            pltpu.VMEM((ROWS, WROWS), BF16),
            pltpu.VMEM((PART, WROWS, HALF), BF16),
            pltpu.VMEM((PART, WROWS, HALF), BF16),
            pltpu.VMEM((ROWS * 8, SIDE), BF16),
            pltpu.VMEM((CTX, 2 * BLOCK, SIDE), BF16),
            pltpu.VMEM((ROWS, SLAB), BF16),
            pltpu.VMEM((PART, CTX, BLOCK, SIDE), BF16),
            pltpu.VMEM((PART, CTX, BLOCK, SIDE), BF16),
            pltpu.VMEM((OWN, SIDE, SIDE), F32),
            pltpu.VMEM((OWN // 2, 2 * SIDE, 2 * SIDE), F32),
            pltpu.VMEM((PART, CTX, BLOCK, SIDE), BF16),
            pltpu.VMEM((PART, CTX, BLOCK, SIDE), BF16),
            pltpu.VMEM((3, 8, ROWS), F32),
            pltpu.VMEM((3, SIDE, ROWS), F32),
            pltpu.VMEM((3, ROWS, SIDE), F32),
            pltpu.VMEM((SIDE, ROWS), F32),
            pltpu.VMEM((ROWS, SIDE), F32),
            dma((4,)),
            dma((2, 9)), dma((2, 9)),
            dma((2, 9)), dma((2, 9)),
            dma((9,)), dma((9,)),
            dma((3, 9)), dma((3, 9)),
            dma((8,)), dma((8,)),
            dma((8,)), dma((8,)),
            dma((4,)),
            dma((4,)),
            dma((CTX,)), dma((CTX,)),
            dma((PART, CTX)), dma((PART, CTX)),
            dma((PART, CTX)), dma((PART, CTX)),
        ],
        compiler_params=pltpu.CompilerParams(
            collective_id=0, has_side_effects=True, vmem_limit_bytes=62 * 2**20
        ),
        cost_estimate=pl.CostEstimate(
            flops=2 * (3 * ROWS * TP * ROWS * SLAB + TP * ROWS * ROWS * SLAB) + 2_400_000_000,
            bytes_accessed=8 * 2**20,
            transcendentals=0,
        ),
        name="hyena",
    )(
        tokens,
        in_weight,
        jnp.swapaxes(short_taps, 1, 2),
        long_filter,
        skip_gain.reshape(1, ROWS),
        out_weight,
        *tables(),
    )


def solution(mesh):
    placed = (
        P("tp", "ctx"),
        P(None, "ctx", "tp"),
        P(None, "tp", None),
        P("tp", "ctx"),
        P("tp"),
        P("tp", "ctx"),
    )
    return jax.shard_map(
        per_device, mesh=mesh, in_specs=placed, out_specs=P("tp", "ctx"), check_vma=False
    )
```
